32 devices in a mesh: loop: 8 (over z, core), chan: 4 (over y, x).
Axes of the slice: x: 2, y: 2, z: 4, core: 2. Of those that a mesh axis runs over, the one named last changes fastest.
Arguments:
- features: bfloat16 [32768, 256], P('loop', 'chan'), may hold values from -6 to 6
- kernel_tap_rows: float32 [9, 256], P(None, 'chan'), may hold values from -2 to 2
- in_weight: bfloat16 [256, 1024], replicated, may hold values from -0.375 to 0.375
- out_weight: bfloat16 [1024, 256], replicated, may hold values from -0.1875 to 0.1875
- cotangent: bfloat16 [32768, 256], P('loop', 'chan'), may hold values from -6 to 6
Outputs:
- block_out: bfloat16 [32768, 256], P('loop', 'chan')
- grad_features: bfloat16 [32768, 256], P('loop', 'chan')
- grad_in_weight: float32 [256, 1024], P('chan', 'loop')
- grad_out_weight: float32 [1024, 256], P('loop', 'chan')
- grad_kernel: float32 [9, 256], P(None, 'chan')
The draws below stay inside these ranges and needn't reach their ends.
All inputs are finite; a program needn't handle non-finite values.
Results may differ from the reference program's by a relative error of at most 0.017.
Values may be sent and summed in bfloat16 or wider, within the bound.
A program may use at most 64 MiB of HBM per device.

```python
import math
import jax
import jax.numpy as jnp
from jax import lax

C = 256
F = 1024
TAPS = 9
DILATION_STEP = 512
BASES = 32768


def strengthened(array, rng, source, target, blocks, factor):
    def block_of(position):
        return (jnp.arange(array.shape[position]) // (array.shape[position] // blocks)).reshape((-1,) + (1,) * (array.ndim - 1 - position))

    one_side = jax.random.permutation(rng, blocks)[block_of(target)]
    far = (block_of(target) + blocks // 2) % blocks
    return jnp.where((block_of(source) == one_side) | (block_of(source) == far), factor * array, array)


def levels(stream_key, extent, pieces, smallest, largest):
    def one(position, blocks):
        draws = jax.random.uniform(jax.random.fold_in(jax.random.fold_in(stream_key, 6), position), (blocks,), jnp.float32, smallest / len(pieces), largest / len(pieces))
        return jnp.repeat(jnp.exp(draws), extent[position] // blocks).reshape((-1,) + (1,) * (len(extent) - position - 1))

    gain = one(*pieces[0])
    for cut in pieces[1:]:
        gain = gain * one(*cut)
    return gain


def scatter_about(rng, dims, deviation, bound, cuts=(), dtype=jnp.bfloat16):
    result = jax.random.normal(rng, dims, jnp.float32) * deviation
    if len(cuts) > 0:
        result = levels(rng, dims, cuts, -0.22, 0.18) * result
    return jnp.clip(result, min=-bound, max=bound).astype(dtype)


def gaussian_with(own_key, extent, width, reach, shards, heavy, held_as=jnp.bfloat16):
    entries = width * jax.random.normal(own_key, extent, jnp.float32)
    if shards:
        entries = entries * levels(own_key, extent, shards, -0.22, 0.18)
    return jnp.clip(strengthened(entries, jax.random.fold_in(own_key, 3), *heavy), -reach, reach).astype(held_as)


def setup_inputs(seed: int = 0) -> dict:
    key_of = jax.random.split(jax.random.key(seed), 6)
    return {
        "features": scatter_about(key_of[0], (BASES, C), 1.0, 6.0, ((0, 8), (1, 4))),
        "kernel_tap_rows": scatter_about(key_of[1], (TAPS, C), TAPS ** -0.5, 2.0, ((1, 4),), jnp.float32),
        "in_weight": scatter_about(key_of[2], (C, F), C ** -0.5, 0.375),
        "out_weight": scatter_about(key_of[3], (F, C), F ** -0.5, 0.1875),
        "cotangent": gaussian_with(key_of[4], (BASES, C), 1.0, 6.0, ((0, 8), (1, 4)), (0, 1, 8, 2.0)),
    }


gelu_scale = math.sqrt(2.0 / math.pi)
cubic_coef = 0.044715
epsilon = 1e-05

def gelu_pair(inputs):
    inner_arg = gelu_scale * (inputs + cubic_coef * inputs * inputs * inputs)
    tangent = jnp.tanh(inner_arg)
    act_value = 0.5 * inputs * (1.0 + tangent)
    act_slope = 0.5 * (1.0 + tangent) + 0.5 * inputs * (1.0 - tangent * tangent) * gelu_scale * (1.0 + 3.0 * cubic_coef * inputs * inputs)
    return (act_value, act_slope)

def reference(features, kernel_tap_rows, in_weight, out_weight, cotangent):
    length = features.shape[0]
    middle_position = (TAPS - 1) // 2
    widened_bases = features.astype(jnp.float32)
    blended_sum = jnp.zeros_like(widened_bases)
    for kernel_tap_index in range(TAPS):
        blended_sum = blended_sum + kernel_tap_rows[kernel_tap_index] * jnp.roll(widened_bases, -(kernel_tap_index - middle_position) * DILATION_STEP, axis=0)
    filtered = blended_sum.astype(jnp.bfloat16)
    block_rows = math.gcd(length, 16384)
    block_count = length // block_rows
    filtered_blocks = filtered.reshape(block_count, block_rows, C)
    upstream_blocks = cotangent.reshape(block_count, block_rows, C)

    def step_block(running, row_pair):
        grad_in_sum, grad_out_sum = running
        row_block, upstream = row_pair
        values = row_block.astype(jnp.float32)
        mean_value = lax.optimization_barrier(jnp.mean(values, axis=-1, keepdims=True))
        centred = values - mean_value
        variance = lax.optimization_barrier(jnp.mean(centred * centred, axis=-1, keepdims=True))
        inv_std = lax.rsqrt(variance + epsilon)
        normed = centred * inv_std
        normed_b = normed.astype(jnp.bfloat16)
        hidden_pre = jnp.dot(normed_b, in_weight, preferred_element_type=jnp.float32)
        act_value, act_slope = gelu_pair(hidden_pre)
        act_b = act_value.astype(jnp.bfloat16)
        branch = jnp.dot(act_b, out_weight, preferred_element_type=jnp.float32).astype(jnp.bfloat16)
        grad_act = jnp.dot(upstream, out_weight.T, preferred_element_type=jnp.float32)
        grad_pre = (grad_act * act_slope).astype(jnp.bfloat16)
        grad_normed = jnp.dot(grad_pre, in_weight.T, preferred_element_type=jnp.float32)
        grad_filtered = inv_std * (grad_normed - lax.optimization_barrier(jnp.mean(grad_normed, axis=-1, keepdims=True)) - normed * lax.optimization_barrier(jnp.mean(grad_normed * normed, axis=-1, keepdims=True)))
        back_rows = grad_filtered.astype(jnp.bfloat16)
        grad_in_sum = grad_in_sum + jnp.dot(normed_b.T, grad_pre, preferred_element_type=jnp.float32)
        grad_out_sum = grad_out_sum + jnp.dot(act_b.T, upstream, preferred_element_type=jnp.float32)
        return ((grad_in_sum, grad_out_sum), (branch, back_rows))
    start_sums = (jnp.zeros((C, F), jnp.float32), jnp.zeros((F, C), jnp.float32))
    (grad_in_sum, grad_out_sum), (branch, back_rows) = lax.scan(step_block, start_sums, (filtered_blocks, upstream_blocks))
    branch = branch.reshape(length, C)
    block_out = (widened_bases + branch.astype(jnp.float32)).astype(jnp.bfloat16)
    back_wide = back_rows.reshape(length, C).astype(jnp.float32)
    grad_sum_rows = cotangent.astype(jnp.float32)
    kernel_rows = []
    for kernel_tap_index in range(TAPS):
        shift_positions = (kernel_tap_index - middle_position) * DILATION_STEP
        grad_sum_rows = grad_sum_rows + kernel_tap_rows[kernel_tap_index] * jnp.roll(back_wide, shift_positions, axis=0)
        kernel_rows.append(lax.optimization_barrier(jnp.sum(back_wide * jnp.roll(widened_bases, -shift_positions, axis=0), axis=0)))
    grad_scale = 1.0 / math.sqrt(length)
    grad_kernel = jnp.stack(kernel_rows) * grad_scale
    return (block_out, grad_sum_rows.astype(jnp.bfloat16), grad_in_sum * grad_scale, grad_out_sum * grad_scale, grad_kernel)
```

```python
import functools
import math

import jax
import jax.numpy as jnp
from jax import lax
from jax.experimental import pallas as pl
from jax.experimental.pallas import tpu as pltpu
from jax.sharding import PartitionSpec as P

TAPS = 9
DILATION_STEP = 512


gelu_scale = math.sqrt(2.0 / math.pi)
cubic_coef = 0.044715
epsilon = 1e-05


def with_halo(cells, sides, width):
    for axis, dim in sides:
        count = lax.axis_size(axis)
        head = lax.slice_in_dim(cells, 0, width, axis=dim)
        tail = lax.slice_in_dim(cells, cells.shape[dim] - width, cells.shape[dim], axis=dim)
        cells = jnp.concatenate(
            [
                lax.ppermute(tail, axis, [(i, (i + 1) % count) for i in range(count)]),
                cells,
                lax.ppermute(head, axis, [((i + 1) % count, i) for i in range(count)]),
            ],
            axis=dim,
        )
    return cells


def gelu_pair(inputs):
    inner_arg = gelu_scale * (inputs + cubic_coef * inputs * inputs * inputs)
    tangent = jnp.tanh(inner_arg)
    act_value = 0.5 * inputs * (1.0 + tangent)
    act_slope = 0.5 * (1.0 + tangent) + 0.5 * inputs * (1.0 - tangent * tangent) * gelu_scale * (
        1.0 + 3.0 * cubic_coef * inputs * inputs
    )
    return (act_value, act_slope)


def widen_rows(field_rows, reach_positions):
    return with_halo(field_rows, (("loop", 0),), reach_positions)


def shards(features, kernel_tap_rows, in_weight, out_weight, cotangent):
    middle_position = (TAPS - 1) // 2
    reach_positions = middle_position * DILATION_STEP
    loop_size = lax.axis_size("loop")
    chan_size = lax.axis_size("chan")
    rows_here = features.shape[0]
    grad_scale = 1.0 / math.sqrt(rows_here * loop_size)
    padded_in = widen_rows(features, reach_positions)
    blended_sum = jnp.zeros(features.shape, jnp.float32)
    for kernel_tap_index in range(TAPS):
        leading_row = reach_positions + (kernel_tap_index - middle_position) * DILATION_STEP
        blended_sum = blended_sum + kernel_tap_rows[kernel_tap_index] * padded_in[
            leading_row : leading_row + rows_here
        ].astype(jnp.float32)
    filtered = blended_sum.astype(jnp.bfloat16)
    row_block, upstream = (
        lax.all_to_all(filtered, "chan", split_axis=0, concat_axis=1, tiled=True),
        lax.all_to_all(cotangent, "chan", split_axis=0, concat_axis=1, tiled=True),
    )
    values = row_block.astype(jnp.float32)
    mean_value = jnp.mean(values, axis=-1, keepdims=True)
    centred = values - mean_value
    variance = jnp.mean(centred * centred, axis=-1, keepdims=True)
    inv_std = lax.rsqrt(variance + epsilon)
    normed = centred * inv_std
    normed_b = normed.astype(jnp.bfloat16)
    hidden_pre = jnp.dot(normed_b, in_weight, preferred_element_type=jnp.float32)
    act_value, act_slope = gelu_pair(hidden_pre)
    act_b = act_value.astype(jnp.bfloat16)
    branch = jnp.dot(act_b, out_weight, preferred_element_type=jnp.float32).astype(jnp.bfloat16)
    grad_act = jnp.einsum("pc,fc->pf", upstream, out_weight, preferred_element_type=jnp.float32)
    grad_pre = (grad_act * act_slope).astype(jnp.bfloat16)
    grad_normed = jnp.einsum("pf,cf->pc", grad_pre, in_weight, preferred_element_type=jnp.float32)
    grad_filtered = inv_std * (
        grad_normed
        - jnp.mean(grad_normed, axis=-1, keepdims=True)
        - normed * jnp.mean(grad_normed * normed, axis=-1, keepdims=True)
    )
    back_rows = grad_filtered.astype(jnp.bfloat16)
    local_rows = row_block.shape[0]
    width_c = row_block.shape[1]
    width_f = hidden_pre.shape[1]
    chan_part = width_c // chan_size
    loop_part = width_f // loop_size
    normed_parts = normed_b.reshape(local_rows, chan_size, chan_part)
    upstream_parts = upstream.reshape(local_rows, chan_size, chan_part)
    grad_parts = grad_pre.reshape(local_rows, loop_size, loop_part)
    act_parts = act_b.reshape(local_rows, loop_size, loop_part)
    term_in = (
        jnp.einsum("pai,pbj->baij", normed_parts, grad_parts, preferred_element_type=jnp.float32)
        * grad_scale
    )
    term_out = (
        jnp.einsum("pbj,pai->baji", act_parts, upstream_parts, preferred_element_type=jnp.float32)
        * grad_scale
    )
    branch_cols, back_cols = (
        lax.all_to_all(branch, "chan", split_axis=1, concat_axis=0, tiled=True),
        lax.all_to_all(back_rows, "chan", split_axis=1, concat_axis=0, tiled=True),
    )
    block_out = (features.astype(jnp.float32) + branch_cols.astype(jnp.float32)).astype(
        jnp.bfloat16
    )
    first_in, first_out = (
        lax.psum_scatter(
            term_in.astype(jnp.bfloat16), "chan", scatter_dimension=1, tiled=True
        ).astype(jnp.float32),
        lax.psum_scatter(
            term_out.astype(jnp.bfloat16), "chan", scatter_dimension=1, tiled=True
        ).astype(jnp.float32),
    )
    summed_in, summed_out = (
        lax.psum_scatter(first_in, "loop", scatter_dimension=0, tiled=True),
        lax.psum_scatter(first_out, "loop", scatter_dimension=0, tiled=True),
    )
    grad_in_weight = summed_in.reshape(chan_part, loop_part)
    grad_out_weight = summed_out.reshape(loop_part, chan_part)
    padded_back = widen_rows(back_cols, reach_positions)
    grad_sum_rows = cotangent.astype(jnp.float32)
    back_wide = back_cols.astype(jnp.float32)
    kernel_rows = []
    for kernel_tap_index in range(TAPS):
        shift_positions = (kernel_tap_index - middle_position) * DILATION_STEP
        first_back = reach_positions - shift_positions
        grad_sum_rows = grad_sum_rows + kernel_tap_rows[kernel_tap_index] * padded_back[
            first_back : first_back + rows_here
        ].astype(jnp.float32)
        first_in_row = reach_positions + shift_positions
        kernel_rows.append(
            jnp.sum(
                back_wide * padded_in[first_in_row : first_in_row + rows_here].astype(jnp.float32),
                axis=0,
            )
        )
    kernel_terms = jnp.stack(kernel_rows) * grad_scale
    grad_kernel = lax.psum(kernel_terms, "loop")
    return (
        block_out,
        grad_sum_rows.astype(jnp.bfloat16),
        grad_in_weight,
        grad_out_weight,
        grad_kernel,
    )


MESH = pl.DeviceIdType.MESH
MIDDLE = (TAPS - 1) // 2
TILE_STEPS = 2
SUB = 64


def fused_kernel(
    L, J, grad_scale,
    x, ct, taps, win, wout,
    bo_out, gx_out, gw_in_out, gw_out_out, gk_out,
    tb, tf, xs, xr, xe, cs, cr, ctf, nb, nrm, istd, act, gp, ge,
    bs, br, gs, gr, gfull, gsend, grecv, hf, hs, hr, sf, tr, kv, kp, kr, kt,
    send, recv,
):
    rows, cl = x.shape
    C = cl * J
    F = win.shape[1]
    R = DILATION_STEP // J
    K = rows // DILATION_STEP
    PAIRS = K // 2
    TILE = 2 * R
    Z = L // 2
    own = MIDDLE * R
    me_l, me_j = lax.axis_index("loop"), lax.axis_index("chan")
    core, z = lax.rem(me_l, 2), me_l // 2
    used = [0]

    def take(n=1):
        used[0] += n
        return used[0] - n

    def rcopy(src, dst, idx, l, j):
        return pltpu.make_async_remote_copy(
            src_ref=src, dst_ref=dst, send_sem=send.at[idx], recv_sem=recv.at[idx],
            device_id=(l, j), device_id_type=MESH)

    chan_peers = [lax.rem(me_j + d, J) for d in range(1, J)]
    loop_peers = [lax.rem(me_l + e, L) for e in range(1, L)]
    right, left = loop_peers[0], loop_peers[-1]

    barrier = pltpu.get_barrier_semaphore()
    for j in chan_peers:
        pl.semaphore_signal(barrier, inc=1, device_id=(me_l, j), device_id_type=MESH)
    for l in loop_peers:
        pl.semaphore_signal(barrier, inc=1, device_id=(l, me_j), device_id_type=MESH)

    def pack(src, dst):
        for m in range(PAIRS):
            for j in range(J):
                a = 2 * m * DILATION_STEP + j * R
                b = a + DILATION_STEP
                dst[j, m * R:(m + 1) * R, :] = jnp.concatenate([src[a:a + R, :], src[b:b + R, :]], axis=1)

    tb[me_j] = jnp.zeros((16, 128), jnp.float32)
    tb[me_j, 0:TAPS, 0:cl] = taps[...]
    pack(x, xs)
    pl.semaphore_wait(barrier, J - 1 + L - 1)

    pending = []

    def to_chan(src, dst):
        out = []
        for j in chan_peers:
            c = rcopy(src.at[j], dst.at[me_j], take(), me_l, j)
            c.start()
            out.append(c)
        pending.extend(out)
        return out

    x_in = to_chan(xs, xr)
    tap_in = []
    for j in chan_peers:
        c = rcopy(tb.at[me_j], tb.at[me_j], take(), me_l, j)
        c.start()
        tap_in.append(c)
    pending.extend(tap_in)
    pack(ct, cs)
    ct_in = to_chan(cs, cr)

    def unpack_full(buf, dst, base, m):
        for h in range(2):
            at = base + (2 * m + h) * R
            dst[at:at + R, :] = jnp.concatenate(
                [buf[s, m * R:(m + 1) * R, h * cl:(h + 1) * cl] for s in range(J)], axis=1)

    xr[me_j] = xs[me_j]
    for c in x_in:
        c.wait_recv()
    half = K // 2 * R
    for m in range(PAIRS // 2):
        unpack_full(xr, xe, own, m)
    x_left = rcopy(xe.at[own:own + own], xe.at[own + K * R:2 * own + K * R], take(), left, me_j)
    x_left.start()
    for m in range(PAIRS // 2, PAIRS):
        unpack_full(xr, xe, own, m)
    x_right = rcopy(xe.at[K * R:own + K * R], xe.at[0:own], take(), right, me_j)
    x_right.start()
    for c in tap_in:
        c.wait_recv()
    tf[...] = jnp.concatenate([tb[s, :, 0:cl] for s in range(J)], axis=1)
    cr[me_j] = cs[me_j]
    for c in ct_in:
        c.wait_recv()
    for m in range(PAIRS):
        unpack_full(cr, ctf, 0, m)
    x_left.wait_recv()
    x_right.wait_recv()
    pending.extend([x_left, x_right])

    bo_base = take(PAIRS * (J - 1))
    ge_left = rcopy(ge.at[own:own + own], ge.at[own + K * R:2 * own + K * R], take(), left, me_j)
    ge_right = rcopy(ge.at[K * R:own + K * R], ge.at[0:own], take(), right, me_j)
    gs_base = take(PAIRS * (J - 1))
    core_base = take(Z)

    def tile_sends(src, dst, base, tile):
        at = pl.ds(pl.multiple_of(tile * R, R), R)
        return [rcopy(src.at[j, at], dst.at[me_j, at], base + tile * (J - 1) + d, me_l, j)
                for d, j in enumerate(chan_peers)]

    def tile_body(tile, carry):
        base = pl.multiple_of(tile * TILE, TILE)
        for b in range(TILE // SUB):
            acc = jnp.zeros((SUB, C), jnp.float32)
            for t in range(TAPS):
                acc = acc + tf[t:t + 1, :] * xe[pl.ds(base + b * SUB + t * R, SUB), :].astype(jnp.float32)
            v = acc.astype(jnp.bfloat16).astype(jnp.float32)
            centred = v - jnp.mean(v, axis=-1, keepdims=True)
            inv = lax.rsqrt(jnp.mean(centred * centred, axis=-1, keepdims=True) + epsilon)
            normed = centred * inv
            nrm[b * SUB:(b + 1) * SUB, :] = normed
            istd[b * SUB:(b + 1) * SUB, :] = inv
            nb[pl.ds(base + b * SUB, SUB), :] = normed.astype(jnp.bfloat16)
        here = pl.ds(base, TILE)
        normed_b = nb[here, :]
        up = ctf[here, :]
        FC = 256
        for f in range(F // FC):
            cols = slice(f * FC, (f + 1) * FC)
            pre = jnp.dot(normed_b, win[:, cols], preferred_element_type=jnp.float32)
            ga = lax.dot_general(up, wout[cols, :], (((1,), (1,)), ((), ())), preferred_element_type=jnp.float32)
            sq = pre * pre
            tangent = jnp.tanh(pre * (gelu_scale + (gelu_scale * cubic_coef) * sq))
            gate = 0.5 + 0.5 * tangent
            slope = gate + pre * (gate * (1.0 - tangent)) * (gelu_scale + (3.0 * gelu_scale * cubic_coef) * sq)
            act[here, cols] = (pre * gate).astype(jnp.bfloat16)
            gp[here, cols] = (ga * slope).astype(jnp.bfloat16)
        gn = lax.dot_general(gp[here, :], win[...], (((1,), (1,)), ((), ())), preferred_element_type=jnp.float32)
        for b in range(TILE // SUB):
            s = slice(b * SUB, (b + 1) * SUB)
            g, normed = gn[s], nrm[s, :]
            out = istd[s, :] * (g - jnp.mean(g, axis=-1, keepdims=True)
                                - normed * jnp.mean(g * normed, axis=-1, keepdims=True))
            ge[pl.ds(own + base + b * SUB, SUB), :] = out.astype(jnp.bfloat16)

        @pl.when(tile == PAIRS // 2 - 1)
        def _():
            ge_left.start()

        @pl.when(tile == PAIRS - 1)
        def _():
            ge_right.start()

        branch = jnp.dot(act[here, :], wout[...], preferred_element_type=jnp.float32).astype(jnp.bfloat16)
        bo = (xe[pl.ds(own + base, TILE), :].astype(jnp.float32) + branch.astype(jnp.float32)).astype(jnp.bfloat16)
        at = pl.ds(pl.multiple_of(tile * R, R), R)
        for j in range(J):
            bs[j, at, :] = jnp.concatenate([bo[0:R, j * cl:(j + 1) * cl], bo[R:, j * cl:(j + 1) * cl]], axis=1)
        for c in tile_sends(bs, br, bo_base, tile):
            c.start()
        return carry

    lax.fori_loop(0, PAIRS, tile_body, 0)

    def term_body(zz, carry):
        cols = pl.ds(pl.multiple_of(zz * 256, 256), 256)
        for i, (a, b) in enumerate(((nb, gp), (ctf, act))):
            term = lax.dot_general(a[...], b[:, cols], (((0,), (0,)), ((), ())),
                                   preferred_element_type=jnp.float32) * grad_scale
            for h in range(2):
                part = term[:, h * 128:(h + 1) * 128]
                gfull[h, zz, i] = part
                gsend[h, zz, i] = part.astype(jnp.bfloat16)
        rcopy(gsend.at[1 - core, zz], grecv.at[zz], core_base + zz, z * 2 + 1 - core, me_j).start()
        return carry

    lax.fori_loop(0, Z, term_body, 0)

    def kernel_body(blk, carry):
        base = pl.multiple_of(blk * SUB, SUB)
        g = ge[pl.ds(own + base, SUB), :].astype(jnp.float32)
        return tuple(
            carry[t] + jnp.sum((g * xe[pl.ds(base + t * R, SUB), :].astype(jnp.float32)).reshape(SUB // 8, 8, C), axis=0)
            for t in range(TAPS))

    terms = lax.fori_loop(0, K * R // SUB, kernel_body,
                          tuple(jnp.zeros((8, C), jnp.float32) for _ in range(TAPS)))
    kv[...] = jnp.zeros_like(kv)
    for t in range(TAPS):
        kv[t:t + 1, :] = jnp.sum(terms[t], axis=0, keepdims=True) * grad_scale
    for j in range(J):
        kp[j] = jnp.concatenate([kv[:, j * cl:(j + 1) * cl], jnp.zeros((16, 128 - cl), jnp.float32)], axis=1)
    k_in = to_chan(kp, kr)

    ge_left.wait_recv()
    ge_right.wait_recv()
    pending.extend([ge_left, ge_right])

    def back_body(tile, carry):
        base = pl.multiple_of(tile * TILE, TILE)
        for b in range(R // SUB):
            pair = []
            for h in range(2):
                off = base + h * R + b * SUB
                acc = ctf[pl.ds(off, SUB), :].astype(jnp.float32)
                for t in range(TAPS):
                    acc = acc + tf[t:t + 1, :] * ge[pl.ds(off + (TAPS - 1 - t) * R, SUB), :].astype(jnp.float32)
                pair.append(acc.astype(jnp.bfloat16))
            at = pl.ds(pl.multiple_of(tile * R, R) + b * SUB, SUB)
            for j in range(J):
                gs[j, at, :] = jnp.concatenate([p[:, j * cl:(j + 1) * cl] for p in pair], axis=1)
        for c in tile_sends(gs, gr, gs_base, tile):
            c.start()
        return carry

    lax.fori_loop(0, PAIRS, back_body, 0)

    CR = C // J

    def core_sum(zz, carry):
        c = rcopy(gsend.at[1 - core, zz], grecv.at[zz], core_base + zz, z * 2 + 1 - core, me_j)
        c.wait_recv()
        c.wait_send()
        for i in range(2):
            h = gfull[core, zz, i] + grecv[zz, i].astype(jnp.float32)
            for j in range(J):
                hf[j, zz, i] = h[j * CR:(j + 1) * CR]
                hs[j, zz, i] = h[j * CR:(j + 1) * CR].astype(jnp.bfloat16)
        return carry

    lax.fori_loop(0, Z, core_sum, 0)
    h_in = to_chan(hs, hr)
    for c in k_in:
        c.wait_recv()
    total = kp[me_j]
    for d in range(1, J):
        total = total + kr[lax.rem(me_j + J - d, J)]
    kt[me_l] = total
    kt_in = []
    for l in loop_peers:
        c = rcopy(kt.at[me_l], kt.at[me_l], take(), l, me_j)
        c.start()
        kt_in.append(c)
    pending.extend(kt_in)

    def finish(src, buf, base, out):
        buf[me_j] = src[me_j]
        for tile in range(PAIRS):
            for c in tile_sends(src, buf, base, tile):
                c.wait_recv()
                c.wait_send()
        for s in range(J):
            for m in range(PAIRS):
                for h in range(2):
                    at = (2 * m + h) * DILATION_STEP + s * R
                    out[at:at + R, :] = buf[s, m * R:(m + 1) * R, h * cl:(h + 1) * cl]

    finish(bs, br, bo_base, bo_out)
    for c in h_in:
        c.wait_recv()
    for zz in range(Z):
        total = hf[me_j, zz]
        for d in range(1, J):
            total = total + hr[lax.rem(me_j + J - d, J), zz].astype(jnp.float32)
        sf[zz] = total
    z_in = []
    for e in range(1, Z):
        zz = lax.rem(z + e, Z)
        c = rcopy(sf.at[zz], tr.at[z], take(), zz * 2 + core, me_j)
        c.start()
        z_in.append(c)
    pending.extend(z_in)
    finish(gs, gr, gs_base, gx_out)
    for c in kt_in:
        c.wait_recv()
    total = kt[0]
    for l in range(1, L):
        total = total + kt[l]
    gk_out[...] = total[0:TAPS, 0:cl]
    for c in z_in:
        c.wait_recv()
    total = sf[z]
    for e in range(1, Z):
        total = total + tr[lax.rem(z + Z - e, Z)]
    gw_in_out[...] = total[0]
    gw_out_out[...] = total[1].T
    for c in pending:
        c.wait_send()


def fits(L, J, rows, cl, F):
    R = DILATION_STEP // J
    return (cl * 2 == 128 and rows == 2 * MIDDLE * DILATION_STEP and L % 2 == 0 and L > 2 and J > 1
            and F == L * 128 and R % SUB == 0)


def fused_shards(features, kernel_tap_rows, in_weight, out_weight, cotangent):
    L, J = lax.axis_size("loop"), lax.axis_size("chan")
    rows, cl = features.shape
    C, F = in_weight.shape
    if not fits(L, J, rows, cl, F):
        return shards(features, kernel_tap_rows, in_weight, out_weight, cotangent)
    R = DILATION_STEP // J
    K = rows // DILATION_STEP
    N = K * R
    Z = L // 2
    CR = C // J
    bf, f32 = jnp.bfloat16, jnp.float32
    ext = N + 2 * MIDDLE * R
    packed = pltpu.VMEM((J, N // 2, 128), bf)
    scratch = [
        pltpu.VMEM((J, 16, 128), f32),
        pltpu.VMEM((16, C), f32),
        packed, packed,
        pltpu.VMEM((ext, C), bf),
        packed, packed,
        pltpu.VMEM((N, C), bf),
        pltpu.VMEM((N, C), bf),
        pltpu.VMEM((2 * R, C), f32),
        pltpu.VMEM((2 * R, 1), f32),
        pltpu.VMEM((N, F), bf),
        pltpu.VMEM((N, F), bf),
        pltpu.VMEM((ext, C), bf),
        packed, packed,
        packed, packed,
        pltpu.VMEM((2, Z, 2, C, 128), f32),
        pltpu.VMEM((2, Z, 2, C, 128), bf),
        pltpu.VMEM((Z, 2, C, 128), bf),
        pltpu.VMEM((J, Z, 2, CR, 128), f32),
        pltpu.VMEM((J, Z, 2, CR, 128), bf),
        pltpu.VMEM((J, Z, 2, CR, 128), bf),
        pltpu.VMEM((Z, 2, CR, 128), f32),
        pltpu.VMEM((Z, 2, CR, 128), f32),
        pltpu.VMEM((16, C), f32),
        pltpu.VMEM((J, 16, 128), f32),
        pltpu.VMEM((J, 16, 128), f32),
        pltpu.VMEM((L, 16, 128), f32),
    ]
    copies = (J - 1) * 5 + 4 + 2 * (K // 2) * (J - 1) + Z + (L - 1) + (Z - 1)
    scratch += [pltpu.SemaphoreType.DMA((copies,)), pltpu.SemaphoreType.DMA((copies,))]
    vmem = pl.BlockSpec(memory_space=pltpu.VMEM)
    return pl.pallas_call(
        functools.partial(fused_kernel, L, J, 1.0 / math.sqrt(rows * L)),
        out_shape=(
            jax.ShapeDtypeStruct((rows, cl), bf),
            jax.ShapeDtypeStruct((rows, cl), bf),
            jax.ShapeDtypeStruct((CR, F // L), f32),
            jax.ShapeDtypeStruct((F // L, CR), f32),
            jax.ShapeDtypeStruct((TAPS, cl), f32),
        ),
        in_specs=[vmem] * 5,
        out_specs=(vmem,) * 5,
        scratch_shapes=scratch,
        compiler_params=pltpu.CompilerParams(
            collective_id=0, has_side_effects=True, vmem_limit_bytes=50 * 1024 * 1024),
        cost_estimate=pl.CostEstimate(flops=12 * N * C * F, bytes_accessed=8 * rows * cl * 2, transcendentals=N * F),
    )(features, cotangent, kernel_tap_rows, in_weight, out_weight)


def solution(mesh):
    placed = (P("loop", "chan"), P(None, "chan"), P(), P(), P("loop", "chan"))
    return jax.shard_map(
        fused_shards,
        mesh=mesh,
        in_specs=placed,
        out_specs=(
            P("loop", "chan"),
            P("loop", "chan"),
            P("chan", "loop"),
            P("loop", "chan"),
            P(None, "chan"),
        ),
        check_vma=False,
    )
```

```python
import functools
import math

import jax
import jax.numpy as jnp
from jax import lax
from jax.experimental import pallas as pl
from jax.experimental.pallas import tpu as pltpu
from jax.sharding import PartitionSpec as P

TAPS = 9
DILATION_STEP = 512


gelu_scale = math.sqrt(2.0 / math.pi)
cubic_coef = 0.044715
epsilon = 1e-05


def with_halo(cells, sides, width):
    for axis, dim in sides:
        count = lax.axis_size(axis)
        head = lax.slice_in_dim(cells, 0, width, axis=dim)
        tail = lax.slice_in_dim(cells, cells.shape[dim] - width, cells.shape[dim], axis=dim)
        cells = jnp.concatenate(
            [
                lax.ppermute(tail, axis, [(i, (i + 1) % count) for i in range(count)]),
                cells,
                lax.ppermute(head, axis, [((i + 1) % count, i) for i in range(count)]),
            ],
            axis=dim,
        )
    return cells


def gelu_pair(inputs):
    inner_arg = gelu_scale * (inputs + cubic_coef * inputs * inputs * inputs)
    tangent = jnp.tanh(inner_arg)
    act_value = 0.5 * inputs * (1.0 + tangent)
    act_slope = 0.5 * (1.0 + tangent) + 0.5 * inputs * (1.0 - tangent * tangent) * gelu_scale * (
        1.0 + 3.0 * cubic_coef * inputs * inputs
    )
    return (act_value, act_slope)


def widen_rows(field_rows, reach_positions):
    return with_halo(field_rows, (("loop", 0),), reach_positions)


def shards(features, kernel_tap_rows, in_weight, out_weight, cotangent):
    middle_position = (TAPS - 1) // 2
    reach_positions = middle_position * DILATION_STEP
    loop_size = lax.axis_size("loop")
    chan_size = lax.axis_size("chan")
    rows_here = features.shape[0]
    grad_scale = 1.0 / math.sqrt(rows_here * loop_size)
    padded_in = widen_rows(features, reach_positions)
    blended_sum = jnp.zeros(features.shape, jnp.float32)
    for kernel_tap_index in range(TAPS):
        leading_row = reach_positions + (kernel_tap_index - middle_position) * DILATION_STEP
        blended_sum = blended_sum + kernel_tap_rows[kernel_tap_index] * padded_in[
            leading_row : leading_row + rows_here
        ].astype(jnp.float32)
    filtered = blended_sum.astype(jnp.bfloat16)
    row_block, upstream = (
        lax.all_to_all(filtered, "chan", split_axis=0, concat_axis=1, tiled=True),
        lax.all_to_all(cotangent, "chan", split_axis=0, concat_axis=1, tiled=True),
    )
    values = row_block.astype(jnp.float32)
    mean_value = jnp.mean(values, axis=-1, keepdims=True)
    centred = values - mean_value
    variance = jnp.mean(centred * centred, axis=-1, keepdims=True)
    inv_std = lax.rsqrt(variance + epsilon)
    normed = centred * inv_std
    normed_b = normed.astype(jnp.bfloat16)
    hidden_pre = jnp.dot(normed_b, in_weight, preferred_element_type=jnp.float32)
    act_value, act_slope = gelu_pair(hidden_pre)
    act_b = act_value.astype(jnp.bfloat16)
    branch = jnp.dot(act_b, out_weight, preferred_element_type=jnp.float32).astype(jnp.bfloat16)
    grad_act = jnp.einsum("pc,fc->pf", upstream, out_weight, preferred_element_type=jnp.float32)
    grad_pre = (grad_act * act_slope).astype(jnp.bfloat16)
    grad_normed = jnp.einsum("pf,cf->pc", grad_pre, in_weight, preferred_element_type=jnp.float32)
    grad_filtered = inv_std * (
        grad_normed
        - jnp.mean(grad_normed, axis=-1, keepdims=True)
        - normed * jnp.mean(grad_normed * normed, axis=-1, keepdims=True)
    )
    back_rows = grad_filtered.astype(jnp.bfloat16)
    local_rows = row_block.shape[0]
    width_c = row_block.shape[1]
    width_f = hidden_pre.shape[1]
    chan_part = width_c // chan_size
    loop_part = width_f // loop_size
    normed_parts = normed_b.reshape(local_rows, chan_size, chan_part)
    upstream_parts = upstream.reshape(local_rows, chan_size, chan_part)
    grad_parts = grad_pre.reshape(local_rows, loop_size, loop_part)
    act_parts = act_b.reshape(local_rows, loop_size, loop_part)
    term_in = (
        jnp.einsum("pai,pbj->baij", normed_parts, grad_parts, preferred_element_type=jnp.float32)
        * grad_scale
    )
    term_out = (
        jnp.einsum("pbj,pai->baji", act_parts, upstream_parts, preferred_element_type=jnp.float32)
        * grad_scale
    )
    branch_cols, back_cols = (
        lax.all_to_all(branch, "chan", split_axis=1, concat_axis=0, tiled=True),
        lax.all_to_all(back_rows, "chan", split_axis=1, concat_axis=0, tiled=True),
    )
    block_out = (features.astype(jnp.float32) + branch_cols.astype(jnp.float32)).astype(
        jnp.bfloat16
    )
    first_in, first_out = (
        lax.psum_scatter(
            term_in.astype(jnp.bfloat16), "chan", scatter_dimension=1, tiled=True
        ).astype(jnp.float32),
        lax.psum_scatter(
            term_out.astype(jnp.bfloat16), "chan", scatter_dimension=1, tiled=True
        ).astype(jnp.float32),
    )
    summed_in, summed_out = (
        lax.psum_scatter(first_in, "loop", scatter_dimension=0, tiled=True),
        lax.psum_scatter(first_out, "loop", scatter_dimension=0, tiled=True),
    )
    grad_in_weight = summed_in.reshape(chan_part, loop_part)
    grad_out_weight = summed_out.reshape(loop_part, chan_part)
    padded_back = widen_rows(back_cols, reach_positions)
    grad_sum_rows = cotangent.astype(jnp.float32)
    back_wide = back_cols.astype(jnp.float32)
    kernel_rows = []
    for kernel_tap_index in range(TAPS):
        shift_positions = (kernel_tap_index - middle_position) * DILATION_STEP
        first_back = reach_positions - shift_positions
        grad_sum_rows = grad_sum_rows + kernel_tap_rows[kernel_tap_index] * padded_back[
            first_back : first_back + rows_here
        ].astype(jnp.float32)
        first_in_row = reach_positions + shift_positions
        kernel_rows.append(
            jnp.sum(
                back_wide * padded_in[first_in_row : first_in_row + rows_here].astype(jnp.float32),
                axis=0,
            )
        )
    kernel_terms = jnp.stack(kernel_rows) * grad_scale
    grad_kernel = lax.psum(kernel_terms, "loop")
    return (
        block_out,
        grad_sum_rows.astype(jnp.bfloat16),
        grad_in_weight,
        grad_out_weight,
        grad_kernel,
    )


MESH = pl.DeviceIdType.MESH
MIDDLE = (TAPS - 1) // 2
TILE_STEPS = 2


def fused_kernel(
    L, J, grad_scale,
    x, ct, taps, win, wout,
    bo_out, gx_out, gw_in_out, gw_out_out, gk_out,
    tb, tf, wint, woutt, xs, xe, cs, ctf, xr, nb, nrm, istd, act, gp, ge,
    bs, br, gs, gr, gfull, gsend, grecv, hf, hs, hr, sf, tr, kp, kr, kt,
    send, recv,
):
    cl, rows = x.shape
    C = cl * J
    F = win.shape[1]
    R = DILATION_STEP // J
    K = rows // DILATION_STEP
    PAIRS = K // 2
    TILE = 2 * R
    Z = L // 2
    own = MIDDLE * R
    me_l, me_j = lax.axis_index("loop"), lax.axis_index("chan")
    core, z = lax.rem(me_l, 2), me_l // 2
    used = [0]

    def take(n=1):
        used[0] += n
        return used[0] - n

    def rcopy(src, dst, idx, l, j):
        return pltpu.make_async_remote_copy(
            src_ref=src, dst_ref=dst, send_sem=send.at[idx], recv_sem=recv.at[idx],
            device_id=(l, j), device_id_type=MESH)

    chan_peers = [lax.rem(me_j + d, J) for d in range(1, J)]
    loop_peers = [lax.rem(me_l + e, L) for e in range(1, L)]
    right, left = loop_peers[0], loop_peers[-1]

    barrier = pltpu.get_barrier_semaphore()
    for j in chan_peers:
        pl.semaphore_signal(barrier, inc=1, device_id=(me_l, j), device_id_type=MESH)
    for l in loop_peers:
        pl.semaphore_signal(barrier, inc=1, device_id=(l, me_j), device_id_type=MESH)

    def pack(src, dst):
        for k in range(K):
            for j in range(J):
                a = k * DILATION_STEP + j * R
                dst[j, :, k * R:(k + 1) * R] = src[:, a:a + R]

    tb[me_j] = jnp.zeros((16, 128), jnp.float32)
    tb[me_j, 0:TAPS, 0:cl] = taps[...]
    pack(x, xs)
    pl.semaphore_wait(barrier, J - 1 + L - 1)

    pending = []

    def to_chan(src, dst):
        out = []
        for j in chan_peers:
            c = rcopy(src.at[j], dst.at[me_j], take(), me_l, j)
            c.start()
            out.append(c)
        pending.extend(out)
        return out

    x_in = to_chan(xs, xr)
    tap_in = []
    for j in chan_peers:
        c = rcopy(tb.at[me_j], tb.at[me_j], take(), me_l, j)
        c.start()
        tap_in.append(c)
    pending.extend(tap_in)
    pack(ct, cs)
    ct_in = to_chan(cs, ctf)

    wint[...] = win[...].T
    woutt[...] = wout[...].T
    xr[me_j] = xs[me_j]
    for c in x_in:
        c.wait_recv()
    for s in range(J):
        xe[s * cl:(s + 1) * cl, own:own + K * R] = xr[s]
    x_left = rcopy(xe.at[:, own:own + own], xe.at[:, own + K * R:2 * own + K * R], take(), left, me_j)
    x_left.start()
    x_right = rcopy(xe.at[:, K * R:own + K * R], xe.at[:, 0:own], take(), right, me_j)
    x_right.start()
    for c in tap_in:
        c.wait_recv()
    columns = jnp.concatenate(
        [jnp.concatenate([tb[s, :, 0:cl] for s in range(J)], axis=1), jnp.zeros((112, C), jnp.float32)], axis=0).T
    for t in range(TAPS):
        tf[t] = jnp.broadcast_to(columns[:, t:t + 1], (C, R))
    ctf[me_j] = cs[me_j]
    for c in ct_in:
        c.wait_recv()
    x_left.wait_recv()
    x_right.wait_recv()
    pending.extend([x_left, x_right])

    bo_base = take(PAIRS * (J - 1))
    ge_left = rcopy(ge.at[:, own:own + own], ge.at[:, own + K * R:2 * own + K * R], take(), left, me_j)
    ge_right = rcopy(ge.at[:, K * R:own + K * R], ge.at[:, 0:own], take(), right, me_j)
    gs_base = take(PAIRS * (J - 1))
    core_base = take(Z)

    def tile_sends(src, dst, base, tile):
        at = pl.ds(pl.multiple_of(tile * TILE, TILE), TILE)
        return [rcopy(src.at[j, :, at], dst.at[me_j, :, at], base + tile * (J - 1) + d, me_l, j)
                for d, j in enumerate(chan_peers)]

    def tile_body(tile, carry):
        base = pl.multiple_of(tile * TILE, TILE)
        for b in range(TILE_STEPS):
            for j in range(J):
                ch = slice(j * cl, (j + 1) * cl)
                acc = jnp.zeros((cl, R), jnp.float32)
                for t in range(TAPS):
                    acc = acc + tf[t, ch, :] * xe[ch, pl.ds(base + (b + t) * R, R)].astype(jnp.float32)
                nrm[ch, b * R:(b + 1) * R] = acc.astype(jnp.bfloat16).astype(jnp.float32)
            here_b = slice(b * R, (b + 1) * R)
            v = nrm[:, here_b]
            centred = v - jnp.mean(v, axis=0, keepdims=True)
            inv = lax.rsqrt(jnp.mean(centred * centred, axis=0, keepdims=True) + epsilon)
            normed = centred * inv
            nrm[:, here_b] = normed
            istd[:, here_b] = inv
            nb[:, pl.ds(base + b * R, R)] = normed.astype(jnp.bfloat16)
        here = pl.ds(base, TILE)
        normed_b = nb[:, here]
        up = jnp.concatenate([ctf[j, :, here] for j in range(J)], axis=0)
        FC = 256
        for f in range(F // FC):
            part = slice(f * FC, (f + 1) * FC)
            pre = jnp.dot(wint[part, :], normed_b, preferred_element_type=jnp.float32)
            ga = jnp.dot(wout[part, :], up, preferred_element_type=jnp.float32)
            sq = pre * pre
            tangent = jnp.tanh(pre * (gelu_scale + (gelu_scale * cubic_coef) * sq))
            gate = 0.5 + 0.5 * tangent
            slope = gate + pre * (gate * (1.0 - tangent)) * (gelu_scale + (3.0 * gelu_scale * cubic_coef) * sq)
            act[part, here] = (pre * gate).astype(jnp.bfloat16)
            gp[part, here] = (ga * slope).astype(jnp.bfloat16)
        gn = jnp.dot(win[...], gp[:, here], preferred_element_type=jnp.float32)
        for b in range(TILE_STEPS):
            s = slice(b * R, (b + 1) * R)
            g, normed = gn[:, s], nrm[:, s]
            out = istd[:, s] * (g - jnp.mean(g, axis=0, keepdims=True)
                                - normed * jnp.mean(g * normed, axis=0, keepdims=True))
            ge[:, pl.ds(own + base + b * R, R)] = out.astype(jnp.bfloat16)

        @pl.when(tile == PAIRS // 2 - 1)
        def _():
            ge_left.start()

        @pl.when(tile == PAIRS - 1)
        def _():
            ge_right.start()

        branch = jnp.dot(woutt[...], act[:, here], preferred_element_type=jnp.float32).astype(jnp.bfloat16)
        bo = (xe[:, pl.ds(own + base, TILE)].astype(jnp.float32) + branch.astype(jnp.float32)).astype(jnp.bfloat16)
        for j in range(J):
            bs[j, :, here] = bo[j * cl:(j + 1) * cl]
        for c in tile_sends(bs, br, bo_base, tile):
            c.start()
        return carry

    lax.fori_loop(0, PAIRS, tile_body, 0)

    def term_body(zz, carry):
        cols = pl.ds(pl.multiple_of(zz * 256, 256), 256)
        both = jnp.concatenate([ctf[j] for j in range(J)], axis=0)
        for i, (a, b) in enumerate(((nb[...], gp), (both, act))):
            term = lax.dot_general(a, b[cols, :], (((1,), (1,)), ((), ())),
                                   preferred_element_type=jnp.float32) * grad_scale
            for h in range(2):
                part = term[:, h * 128:(h + 1) * 128]
                gfull[h, zz, i] = part
                gsend[h, zz, i] = part.astype(jnp.bfloat16)
        rcopy(gsend.at[1 - core, zz], grecv.at[zz], core_base + zz, z * 2 + 1 - core, me_j).start()
        return carry

    lax.fori_loop(0, Z, term_body, 0)

    for j in range(J):
        ch = slice(j * cl, (j + 1) * cl)
        sums = []
        for t in range(TAPS):
            acc = jnp.zeros((cl, R), jnp.float32)
            for k in range(K):
                acc = acc + (ge[ch, own + k * R:own + (k + 1) * R].astype(jnp.float32)
                             * xe[ch, (k + t) * R:(k + t + 1) * R].astype(jnp.float32))
            sums.append(jnp.sum(acc, axis=1, keepdims=True) * grad_scale)
        kp[j] = jnp.concatenate(sums + [jnp.zeros((cl, 128 - TAPS), jnp.float32)], axis=1)
    k_in = to_chan(kp, kr)

    ge_left.wait_recv()
    ge_right.wait_recv()
    pending.extend([ge_left, ge_right])

    def back_body(tile, carry):
        base = pl.multiple_of(tile * TILE, TILE)
        for h in range(TILE_STEPS):
            off = base + h * R
            for j in range(J):
                ch = slice(j * cl, (j + 1) * cl)
                acc = ctf[j, :, pl.ds(off, R)].astype(jnp.float32)
                for t in range(TAPS):
                    acc = acc + tf[t, ch, :] * ge[ch, pl.ds(off + (TAPS - 1 - t) * R, R)].astype(jnp.float32)
                gs[j, :, pl.ds(off, R)] = acc.astype(jnp.bfloat16)
        for c in tile_sends(gs, gr, gs_base, tile):
            c.start()
        return carry

    lax.fori_loop(0, PAIRS, back_body, 0)

    CR = C // J

    def core_sum(zz, carry):
        c = rcopy(gsend.at[1 - core, zz], grecv.at[zz], core_base + zz, z * 2 + 1 - core, me_j)
        c.wait_recv()
        c.wait_send()
        for i in range(2):
            h = gfull[core, zz, i] + grecv[zz, i].astype(jnp.float32)
            for j in range(J):
                hf[j, zz, i] = h[j * CR:(j + 1) * CR]
                hs[j, zz, i] = h[j * CR:(j + 1) * CR].astype(jnp.bfloat16)
        return carry

    lax.fori_loop(0, Z, core_sum, 0)
    h_in = to_chan(hs, hr)
    for c in k_in:
        c.wait_recv()
    total = kp[me_j]
    for d in range(1, J):
        total = total + kr[lax.rem(me_j + J - d, J)]
    kt[me_l] = total
    kt_in = []
    for l in loop_peers:
        c = rcopy(kt.at[me_l], kt.at[me_l], take(), l, me_j)
        c.start()
        kt_in.append(c)
    pending.extend(kt_in)

    def finish(src, buf, base, out):
        buf[me_j] = src[me_j]
        for tile in range(PAIRS):
            for c in tile_sends(src, buf, base, tile):
                c.wait_recv()
                c.wait_send()
        for s in range(J):
            for k in range(K):
                at = k * DILATION_STEP + s * R
                out[:, at:at + R] = buf[s, :, k * R:(k + 1) * R]

    finish(bs, br, bo_base, bo_out)
    for c in h_in:
        c.wait_recv()
    for zz in range(Z):
        total = hf[me_j, zz]
        for d in range(1, J):
            total = total + hr[lax.rem(me_j + J - d, J), zz].astype(jnp.float32)
        sf[zz] = total
    z_in = []
    for e in range(1, Z):
        zz = lax.rem(z + e, Z)
        c = rcopy(sf.at[zz], tr.at[z], take(), zz * 2 + core, me_j)
        c.start()
        z_in.append(c)
    pending.extend(z_in)
    finish(gs, gr, gs_base, gx_out)
    for c in kt_in:
        c.wait_recv()
    total = kt[0]
    for l in range(1, L):
        total = total + kt[l]
    gk_out[...] = total.T[0:TAPS, :]
    for c in z_in:
        c.wait_recv()
    total = sf[z]
    for e in range(1, Z):
        total = total + tr[lax.rem(z + Z - e, Z)]
    gw_in_out[...] = total[0]
    gw_out_out[...] = total[1]
    for c in pending:
        c.wait_send()


def fits(L, J, rows, cl, F):
    R = DILATION_STEP // J
    return (cl * 2 == 128 and rows == 2 * MIDDLE * DILATION_STEP and L % 2 == 0 and L > 2 and J > 1
            and F == L * 128 and R == 128)


def fused_shards(features, kernel_tap_rows, in_weight, out_weight, cotangent):
    L, J = lax.axis_size("loop"), lax.axis_size("chan")
    rows, cl = features.shape
    C, F = in_weight.shape
    if not fits(L, J, rows, cl, F):
        return shards(features, kernel_tap_rows, in_weight, out_weight, cotangent)
    R = DILATION_STEP // J
    K = rows // DILATION_STEP
    N = K * R
    Z = L // 2
    CR = C // J
    bf, f32 = jnp.bfloat16, jnp.float32
    ext = N + 2 * MIDDLE * R
    packed = pltpu.VMEM((J, cl, N), bf)
    scratch = [
        pltpu.VMEM((J, 16, 128), f32),
        pltpu.VMEM((TAPS, C, R), f32),
        pltpu.VMEM((F, C), bf),
        pltpu.VMEM((C, F), bf),
        packed,
        pltpu.VMEM((C, ext), bf),
        packed, packed, packed,
        pltpu.VMEM((C, N), bf),
        pltpu.VMEM((C, 2 * R), f32),
        pltpu.VMEM((1, 2 * R), f32),
        pltpu.VMEM((F, N), bf),
        pltpu.VMEM((F, N), bf),
        pltpu.VMEM((C, ext), bf),
        packed, packed,
        packed, packed,
        pltpu.VMEM((2, Z, 2, C, 128), f32),
        pltpu.VMEM((2, Z, 2, C, 128), bf),
        pltpu.VMEM((Z, 2, C, 128), bf),
        pltpu.VMEM((J, Z, 2, CR, 128), f32),
        pltpu.VMEM((J, Z, 2, CR, 128), bf),
        pltpu.VMEM((J, Z, 2, CR, 128), bf),
        pltpu.VMEM((Z, 2, CR, 128), f32),
        pltpu.VMEM((Z, 2, CR, 128), f32),
        pltpu.VMEM((J, cl, 128), f32),
        pltpu.VMEM((J, cl, 128), f32),
        pltpu.VMEM((L, cl, 128), f32),
    ]
    copies = (J - 1) * 5 + 4 + 2 * (K // 2) * (J - 1) + Z + (L - 1) + (Z - 1)
    scratch += [pltpu.SemaphoreType.DMA((copies,)), pltpu.SemaphoreType.DMA((copies,))]
    vmem = pl.BlockSpec(memory_space=pltpu.VMEM)
    bo, gx, gw_in, gw_out, gk = pl.pallas_call(
        functools.partial(fused_kernel, L, J, 1.0 / math.sqrt(rows * L)),
        out_shape=(
            jax.ShapeDtypeStruct((cl, rows), bf),
            jax.ShapeDtypeStruct((cl, rows), bf),
            jax.ShapeDtypeStruct((CR, F // L), f32),
            jax.ShapeDtypeStruct((CR, F // L), f32),
            jax.ShapeDtypeStruct((TAPS, cl), f32),
        ),
        in_specs=[vmem] * 5,
        out_specs=(vmem,) * 5,
        scratch_shapes=scratch,
        compiler_params=pltpu.CompilerParams(
            collective_id=0, has_side_effects=True, vmem_limit_bytes=50 * 1024 * 1024),
        cost_estimate=pl.CostEstimate(flops=12 * N * C * F, bytes_accessed=8 * rows * cl * 2, transcendentals=N * F),
    )(features.T, cotangent.T, kernel_tap_rows, in_weight, out_weight)
    return bo.T, gx.T, gw_in, gw_out.T, gk


def solution(mesh):
    placed = (P("loop", "chan"), P(None, "chan"), P(), P(), P("loop", "chan"))
    return jax.shard_map(
        fused_shards,
        mesh=mesh,
        in_specs=placed,
        out_specs=(
            P("loop", "chan"),
            P("loop", "chan"),
            P("chan", "loop"),
            P("loop", "chan"),
            P(None, "chan"),
        ),
        check_vma=False,
    )
```

```python
import functools
import math

import jax
import jax.numpy as jnp
from jax import lax
from jax.experimental import pallas as pl
from jax.experimental.pallas import tpu as pltpu
from jax.sharding import PartitionSpec as P

TAPS = 9
DILATION_STEP = 512


gelu_scale = math.sqrt(2.0 / math.pi)
cubic_coef = 0.044715
epsilon = 1e-05


def with_halo(cells, sides, width):
    for axis, dim in sides:
        count = lax.axis_size(axis)
        head = lax.slice_in_dim(cells, 0, width, axis=dim)
        tail = lax.slice_in_dim(cells, cells.shape[dim] - width, cells.shape[dim], axis=dim)
        cells = jnp.concatenate(
            [
                lax.ppermute(tail, axis, [(i, (i + 1) % count) for i in range(count)]),
                cells,
                lax.ppermute(head, axis, [((i + 1) % count, i) for i in range(count)]),
            ],
            axis=dim,
        )
    return cells


def gelu_pair(inputs):
    inner_arg = gelu_scale * (inputs + cubic_coef * inputs * inputs * inputs)
    tangent = jnp.tanh(inner_arg)
    act_value = 0.5 * inputs * (1.0 + tangent)
    act_slope = 0.5 * (1.0 + tangent) + 0.5 * inputs * (1.0 - tangent * tangent) * gelu_scale * (
        1.0 + 3.0 * cubic_coef * inputs * inputs
    )
    return (act_value, act_slope)


def widen_rows(field_rows, reach_positions):
    return with_halo(field_rows, (("loop", 0),), reach_positions)


def shards(features, kernel_tap_rows, in_weight, out_weight, cotangent):
    middle_position = (TAPS - 1) // 2
    reach_positions = middle_position * DILATION_STEP
    loop_size = lax.axis_size("loop")
    chan_size = lax.axis_size("chan")
    rows_here = features.shape[0]
    grad_scale = 1.0 / math.sqrt(rows_here * loop_size)
    padded_in = widen_rows(features, reach_positions)
    blended_sum = jnp.zeros(features.shape, jnp.float32)
    for kernel_tap_index in range(TAPS):
        leading_row = reach_positions + (kernel_tap_index - middle_position) * DILATION_STEP
        blended_sum = blended_sum + kernel_tap_rows[kernel_tap_index] * padded_in[
            leading_row : leading_row + rows_here
        ].astype(jnp.float32)
    filtered = blended_sum.astype(jnp.bfloat16)
    row_block, upstream = (
        lax.all_to_all(filtered, "chan", split_axis=0, concat_axis=1, tiled=True),
        lax.all_to_all(cotangent, "chan", split_axis=0, concat_axis=1, tiled=True),
    )
    values = row_block.astype(jnp.float32)
    mean_value = jnp.mean(values, axis=-1, keepdims=True)
    centred = values - mean_value
    variance = jnp.mean(centred * centred, axis=-1, keepdims=True)
    inv_std = lax.rsqrt(variance + epsilon)
    normed = centred * inv_std
    normed_b = normed.astype(jnp.bfloat16)
    hidden_pre = jnp.dot(normed_b, in_weight, preferred_element_type=jnp.float32)
    act_value, act_slope = gelu_pair(hidden_pre)
    act_b = act_value.astype(jnp.bfloat16)
    branch = jnp.dot(act_b, out_weight, preferred_element_type=jnp.float32).astype(jnp.bfloat16)
    grad_act = jnp.einsum("pc,fc->pf", upstream, out_weight, preferred_element_type=jnp.float32)
    grad_pre = (grad_act * act_slope).astype(jnp.bfloat16)
    grad_normed = jnp.einsum("pf,cf->pc", grad_pre, in_weight, preferred_element_type=jnp.float32)
    grad_filtered = inv_std * (
        grad_normed
        - jnp.mean(grad_normed, axis=-1, keepdims=True)
        - normed * jnp.mean(grad_normed * normed, axis=-1, keepdims=True)
    )
    back_rows = grad_filtered.astype(jnp.bfloat16)
    local_rows = row_block.shape[0]
    width_c = row_block.shape[1]
    width_f = hidden_pre.shape[1]
    chan_part = width_c // chan_size
    loop_part = width_f // loop_size
    normed_parts = normed_b.reshape(local_rows, chan_size, chan_part)
    upstream_parts = upstream.reshape(local_rows, chan_size, chan_part)
    grad_parts = grad_pre.reshape(local_rows, loop_size, loop_part)
    act_parts = act_b.reshape(local_rows, loop_size, loop_part)
    term_in = (
        jnp.einsum("pai,pbj->baij", normed_parts, grad_parts, preferred_element_type=jnp.float32)
        * grad_scale
    )
    term_out = (
        jnp.einsum("pbj,pai->baji", act_parts, upstream_parts, preferred_element_type=jnp.float32)
        * grad_scale
    )
    branch_cols, back_cols = (
        lax.all_to_all(branch, "chan", split_axis=1, concat_axis=0, tiled=True),
        lax.all_to_all(back_rows, "chan", split_axis=1, concat_axis=0, tiled=True),
    )
    block_out = (features.astype(jnp.float32) + branch_cols.astype(jnp.float32)).astype(
        jnp.bfloat16
    )
    first_in, first_out = (
        lax.psum_scatter(
            term_in.astype(jnp.bfloat16), "chan", scatter_dimension=1, tiled=True
        ).astype(jnp.float32),
        lax.psum_scatter(
            term_out.astype(jnp.bfloat16), "chan", scatter_dimension=1, tiled=True
        ).astype(jnp.float32),
    )
    summed_in, summed_out = (
        lax.psum_scatter(first_in, "loop", scatter_dimension=0, tiled=True),
        lax.psum_scatter(first_out, "loop", scatter_dimension=0, tiled=True),
    )
    grad_in_weight = summed_in.reshape(chan_part, loop_part)
    grad_out_weight = summed_out.reshape(loop_part, chan_part)
    padded_back = widen_rows(back_cols, reach_positions)
    grad_sum_rows = cotangent.astype(jnp.float32)
    back_wide = back_cols.astype(jnp.float32)
    kernel_rows = []
    for kernel_tap_index in range(TAPS):
        shift_positions = (kernel_tap_index - middle_position) * DILATION_STEP
        first_back = reach_positions - shift_positions
        grad_sum_rows = grad_sum_rows + kernel_tap_rows[kernel_tap_index] * padded_back[
            first_back : first_back + rows_here
        ].astype(jnp.float32)
        first_in_row = reach_positions + shift_positions
        kernel_rows.append(
            jnp.sum(
                back_wide * padded_in[first_in_row : first_in_row + rows_here].astype(jnp.float32),
                axis=0,
            )
        )
    kernel_terms = jnp.stack(kernel_rows) * grad_scale
    grad_kernel = lax.psum(kernel_terms, "loop")
    return (
        block_out,
        grad_sum_rows.astype(jnp.bfloat16),
        grad_in_weight,
        grad_out_weight,
        grad_kernel,
    )


MESH = pl.DeviceIdType.MESH
MIDDLE = (TAPS - 1) // 2
TILE_STEPS = 2


def fused_kernel(
    L, J, grad_scale,
    x_hbm, ct_hbm, taps_hbm, win_hbm, wout_hbm,
    bo_out, gx_out, gw_in_out, gw_out_out, gk_out,
    tb, tf, wint, woutt, xs, xe, cs, ctf, xr, nb, nrm, istd, act, gp, ge,
    bs, br, gs, gr, gfull, gsend, grecv, hf, hs, hr, sf, tr, kp, kr, kt,
    x, ct, taps, win, wout, load, send, recv,
):
    loads = [pltpu.make_async_copy(a, b, load.at[i]) for i, (a, b) in enumerate(
        ((x_hbm, x), (taps_hbm, taps), (ct_hbm, ct), (win_hbm, win), (wout_hbm, wout)))]
    for c in loads:
        c.start()
    cl, rows = x.shape
    C = cl * J
    F = win.shape[1]
    R = DILATION_STEP // J
    K = rows // DILATION_STEP
    PAIRS = K // 2
    TILE = 2 * R
    Z = L // 2
    own = MIDDLE * R
    me_l, me_j = lax.axis_index("loop"), lax.axis_index("chan")
    core, z = lax.rem(me_l, 2), me_l // 2
    used = [0]

    def take(n=1):
        used[0] += n
        return used[0] - n

    def rcopy(src, dst, idx, l, j):
        return pltpu.make_async_remote_copy(
            src_ref=src, dst_ref=dst, send_sem=send.at[idx], recv_sem=recv.at[idx],
            device_id=(l, j), device_id_type=MESH)

    chan_peers = [lax.rem(me_j + d, J) for d in range(1, J)]
    loop_peers = [lax.rem(me_l + e, L) for e in range(1, L)]
    right, left = loop_peers[0], loop_peers[-1]

    barrier = pltpu.get_barrier_semaphore()
    for j in chan_peers:
        pl.semaphore_signal(barrier, inc=1, device_id=(me_l, j), device_id_type=MESH)
    for l in loop_peers:
        pl.semaphore_signal(barrier, inc=1, device_id=(l, me_j), device_id_type=MESH)

    def pack(src, dst):
        for k in range(K):
            for j in range(J):
                a = k * DILATION_STEP + j * R
                dst[j, :, k * R:(k + 1) * R] = src[:, a:a + R]

    loads[0].wait()
    loads[1].wait()
    tb[me_j] = jnp.zeros((16, 128), jnp.float32)
    tb[me_j, 0:TAPS, 0:cl] = taps[...]
    pack(x, xs)
    pl.semaphore_wait(barrier, J - 1 + L - 1)

    pending = []

    def to_chan(src, dst):
        out = []
        for j in chan_peers:
            c = rcopy(src.at[j], dst.at[me_j], take(), me_l, j)
            c.start()
            out.append(c)
        pending.extend(out)
        return out

    x_in = to_chan(xs, xr)
    tap_in = []
    for j in chan_peers:
        c = rcopy(tb.at[me_j], tb.at[me_j], take(), me_l, j)
        c.start()
        tap_in.append(c)
    pending.extend(tap_in)
    loads[2].wait()
    pack(ct, cs)
    ct_in = to_chan(cs, ctf)

    loads[3].wait()
    loads[4].wait()
    wint[...] = win[...].T
    woutt[...] = wout[...].T
    xr[me_j] = xs[me_j]
    for c in x_in:
        c.wait_recv()
    for s in range(J):
        xe[s * cl:(s + 1) * cl, own:own + K * R] = xr[s]
    x_left = rcopy(xe.at[:, own:own + own], xe.at[:, own + K * R:2 * own + K * R], take(), left, me_j)
    x_left.start()
    x_right = rcopy(xe.at[:, K * R:own + K * R], xe.at[:, 0:own], take(), right, me_j)
    x_right.start()
    for c in tap_in:
        c.wait_recv()
    columns = jnp.concatenate(
        [jnp.concatenate([tb[s, :, 0:cl] for s in range(J)], axis=1), jnp.zeros((112, C), jnp.float32)], axis=0).T
    for t in range(TAPS):
        tf[t] = jnp.broadcast_to(columns[:, t:t + 1], (C, R))
    ctf[me_j] = cs[me_j]
    for c in ct_in:
        c.wait_recv()
    x_left.wait_recv()
    x_right.wait_recv()
    pending.extend([x_left, x_right])

    bo_base = take(PAIRS * (J - 1))
    ge_left = rcopy(ge.at[:, own:own + own], ge.at[:, own + K * R:2 * own + K * R], take(), left, me_j)
    ge_right = rcopy(ge.at[:, K * R:own + K * R], ge.at[:, 0:own], take(), right, me_j)
    gs_base = take(PAIRS * (J - 1))
    core_base = take(Z)

    def tile_sends(src, dst, base, tile):
        at = pl.ds(pl.multiple_of(tile * TILE, TILE), TILE)
        return [rcopy(src.at[j, :, at], dst.at[me_j, :, at], base + tile * (J - 1) + d, me_l, j)
                for d, j in enumerate(chan_peers)]

    def tile_body(tile, carry):
        base = pl.multiple_of(tile * TILE, TILE)
        for b in range(TILE_STEPS):
            for j in range(J):
                ch = slice(j * cl, (j + 1) * cl)
                acc = jnp.zeros((cl, R), jnp.float32)
                for t in range(TAPS):
                    acc = acc + tf[t, ch, :] * xe[ch, pl.ds(base + (b + t) * R, R)].astype(jnp.float32)
                nrm[ch, b * R:(b + 1) * R] = acc.astype(jnp.bfloat16).astype(jnp.float32)
            here_b = slice(b * R, (b + 1) * R)
            v = nrm[:, here_b]
            centred = v - jnp.mean(v, axis=0, keepdims=True)
            inv = lax.rsqrt(jnp.mean(centred * centred, axis=0, keepdims=True) + epsilon)
            normed = centred * inv
            nrm[:, here_b] = normed
            istd[:, here_b] = inv
            nb[:, pl.ds(base + b * R, R)] = normed.astype(jnp.bfloat16)
        here = pl.ds(base, TILE)
        normed_b = nb[:, here]
        up = jnp.concatenate([ctf[j, :, here] for j in range(J)], axis=0)
        FC = 256
        for f in range(F // FC):
            part = slice(f * FC, (f + 1) * FC)
            pre = jnp.dot(wint[part, :], normed_b, preferred_element_type=jnp.float32)
            ga = jnp.dot(wout[part, :], up, preferred_element_type=jnp.float32)
            sq = pre * pre
            tangent = jnp.tanh(pre * (gelu_scale + (gelu_scale * cubic_coef) * sq))
            gate = 0.5 + 0.5 * tangent
            slope = gate + pre * (gate * (1.0 - tangent)) * (gelu_scale + (3.0 * gelu_scale * cubic_coef) * sq)
            act[part, here] = (pre * gate).astype(jnp.bfloat16)
            gp[part, here] = (ga * slope).astype(jnp.bfloat16)
        gn = jnp.dot(win[...], gp[:, here], preferred_element_type=jnp.float32)
        for b in range(TILE_STEPS):
            s = slice(b * R, (b + 1) * R)
            g, normed = gn[:, s], nrm[:, s]
            out = istd[:, s] * (g - jnp.mean(g, axis=0, keepdims=True)
                                - normed * jnp.mean(g * normed, axis=0, keepdims=True))
            ge[:, pl.ds(own + base + b * R, R)] = out.astype(jnp.bfloat16)

        @pl.when(tile == PAIRS // 2 - 1)
        def _():
            ge_left.start()

        @pl.when(tile == PAIRS - 1)
        def _():
            ge_right.start()

        branch = jnp.dot(woutt[...], act[:, here], preferred_element_type=jnp.float32).astype(jnp.bfloat16)
        bo = (xe[:, pl.ds(own + base, TILE)].astype(jnp.float32) + branch.astype(jnp.float32)).astype(jnp.bfloat16)
        for j in range(J):
            bs[j, :, here] = bo[j * cl:(j + 1) * cl]
        for c in tile_sends(bs, br, bo_base, tile):
            c.start()
        return carry

    lax.fori_loop(0, PAIRS, tile_body, 0)

    def term_body(zz, carry):
        cols = pl.ds(pl.multiple_of(zz * 256, 256), 256)
        both = jnp.concatenate([ctf[j] for j in range(J)], axis=0)
        for i, (a, b) in enumerate(((nb[...], gp), (both, act))):
            term = lax.dot_general(a, b[cols, :], (((1,), (1,)), ((), ())),
                                   preferred_element_type=jnp.float32) * grad_scale
            for h in range(2):
                part = term[:, h * 128:(h + 1) * 128]
                gfull[h, zz, i] = part
                gsend[h, zz, i] = part.astype(jnp.bfloat16)
        rcopy(gsend.at[1 - core, zz], grecv.at[zz], core_base + zz, z * 2 + 1 - core, me_j).start()
        return carry

    lax.fori_loop(0, Z, term_body, 0)

    for j in range(J):
        ch = slice(j * cl, (j + 1) * cl)
        sums = []
        for t in range(TAPS):
            acc = jnp.zeros((cl, R), jnp.float32)
            for k in range(K):
                acc = acc + (ge[ch, own + k * R:own + (k + 1) * R].astype(jnp.float32)
                             * xe[ch, (k + t) * R:(k + t + 1) * R].astype(jnp.float32))
            sums.append(jnp.sum(acc, axis=1, keepdims=True) * grad_scale)
        kp[j] = jnp.concatenate(sums + [jnp.zeros((cl, 128 - TAPS), jnp.float32)], axis=1)
    k_in = to_chan(kp, kr)

    ge_left.wait_recv()
    ge_right.wait_recv()
    pending.extend([ge_left, ge_right])

    def back_body(tile, carry):
        base = pl.multiple_of(tile * TILE, TILE)
        for h in range(TILE_STEPS):
            off = base + h * R
            for j in range(J):
                ch = slice(j * cl, (j + 1) * cl)
                acc = ctf[j, :, pl.ds(off, R)].astype(jnp.float32)
                for t in range(TAPS):
                    acc = acc + tf[t, ch, :] * ge[ch, pl.ds(off + (TAPS - 1 - t) * R, R)].astype(jnp.float32)
                gs[j, :, pl.ds(off, R)] = acc.astype(jnp.bfloat16)
        for c in tile_sends(gs, gr, gs_base, tile):
            c.start()
        return carry

    lax.fori_loop(0, PAIRS, back_body, 0)

    CR = C // J

    def core_sum(zz, carry):
        c = rcopy(gsend.at[1 - core, zz], grecv.at[zz], core_base + zz, z * 2 + 1 - core, me_j)
        c.wait_recv()
        c.wait_send()
        for i in range(2):
            h = gfull[core, zz, i] + grecv[zz, i].astype(jnp.float32)
            for j in range(J):
                hf[j, zz, i] = h[j * CR:(j + 1) * CR]
                hs[j, zz, i] = h[j * CR:(j + 1) * CR].astype(jnp.bfloat16)
        return carry

    lax.fori_loop(0, Z, core_sum, 0)
    h_in = to_chan(hs, hr)
    for c in k_in:
        c.wait_recv()
    total = kp[me_j]
    for d in range(1, J):
        total = total + kr[lax.rem(me_j + J - d, J)]
    kt[me_l] = total
    kt_in = []
    for l in loop_peers:
        c = rcopy(kt.at[me_l], kt.at[me_l], take(), l, me_j)
        c.start()
        kt_in.append(c)
    pending.extend(kt_in)

    def finish(src, buf, base, out):
        buf[me_j] = src[me_j]
        for tile in range(PAIRS):
            for c in tile_sends(src, buf, base, tile):
                c.wait_recv()
                c.wait_send()
        for s in range(J):
            for k in range(K):
                at = k * DILATION_STEP + s * R
                out[:, at:at + R] = buf[s, :, k * R:(k + 1) * R]

    finish(bs, br, bo_base, bo_out)
    for c in h_in:
        c.wait_recv()
    for zz in range(Z):
        total = hf[me_j, zz]
        for d in range(1, J):
            total = total + hr[lax.rem(me_j + J - d, J), zz].astype(jnp.float32)
        sf[zz] = total
    z_in = []
    for e in range(1, Z):
        zz = lax.rem(z + e, Z)
        c = rcopy(sf.at[zz], tr.at[z], take(), zz * 2 + core, me_j)
        c.start()
        z_in.append(c)
    pending.extend(z_in)
    finish(gs, gr, gs_base, gx_out)
    for c in kt_in:
        c.wait_recv()
    total = kt[0]
    for l in range(1, L):
        total = total + kt[l]
    gk_out[...] = total.T[0:TAPS, :]
    for c in z_in:
        c.wait_recv()
    total = sf[z]
    for e in range(1, Z):
        total = total + tr[lax.rem(z + Z - e, Z)]
    gw_in_out[...] = total[0]
    gw_out_out[...] = total[1]
    for c in pending:
        c.wait_send()


def fits(L, J, rows, cl, F):
    R = DILATION_STEP // J
    return (cl * 2 == 128 and rows == 2 * MIDDLE * DILATION_STEP and L % 2 == 0 and L > 2 and J > 1
            and F == L * 128 and R == 128)


def fused_shards(features, kernel_tap_rows, in_weight, out_weight, cotangent):
    L, J = lax.axis_size("loop"), lax.axis_size("chan")
    rows, cl = features.shape
    C, F = in_weight.shape
    if not fits(L, J, rows, cl, F):
        return shards(features, kernel_tap_rows, in_weight, out_weight, cotangent)
    R = DILATION_STEP // J
    K = rows // DILATION_STEP
    N = K * R
    Z = L // 2
    CR = C // J
    bf, f32 = jnp.bfloat16, jnp.float32
    ext = N + 2 * MIDDLE * R
    packed = pltpu.VMEM((J, cl, N), bf)
    scratch = [
        pltpu.VMEM((J, 16, 128), f32),
        pltpu.VMEM((TAPS, C, R), f32),
        pltpu.VMEM((F, C), bf),
        pltpu.VMEM((C, F), bf),
        packed,
        pltpu.VMEM((C, ext), bf),
        packed, packed, packed,
        pltpu.VMEM((C, N), bf),
        pltpu.VMEM((C, 2 * R), f32),
        pltpu.VMEM((1, 2 * R), f32),
        pltpu.VMEM((F, N), bf),
        pltpu.VMEM((F, N), bf),
        pltpu.VMEM((C, ext), bf),
        packed, packed,
        packed, packed,
        pltpu.VMEM((2, Z, 2, C, 128), f32),
        pltpu.VMEM((2, Z, 2, C, 128), bf),
        pltpu.VMEM((Z, 2, C, 128), bf),
        pltpu.VMEM((J, Z, 2, CR, 128), f32),
        pltpu.VMEM((J, Z, 2, CR, 128), bf),
        pltpu.VMEM((J, Z, 2, CR, 128), bf),
        pltpu.VMEM((Z, 2, CR, 128), f32),
        pltpu.VMEM((Z, 2, CR, 128), f32),
        pltpu.VMEM((J, cl, 128), f32),
        pltpu.VMEM((J, cl, 128), f32),
        pltpu.VMEM((L, cl, 128), f32),
    ]
    copies = (J - 1) * 5 + 4 + 2 * (K // 2) * (J - 1) + Z + (L - 1) + (Z - 1)
    scratch += [
        pltpu.VMEM((cl, rows), bf),
        pltpu.VMEM((cl, rows), bf),
        pltpu.VMEM((TAPS, cl), f32),
        pltpu.VMEM((C, F), bf),
        pltpu.VMEM((F, C), bf),
        pltpu.SemaphoreType.DMA((5,)),
    ]
    scratch += [pltpu.SemaphoreType.DMA((copies,)), pltpu.SemaphoreType.DMA((copies,))]
    vmem = pl.BlockSpec(memory_space=pltpu.VMEM)
    bo, gx, gw_in, gw_out, gk = pl.pallas_call(
        functools.partial(fused_kernel, L, J, 1.0 / math.sqrt(rows * L)),
        out_shape=(
            jax.ShapeDtypeStruct((cl, rows), bf),
            jax.ShapeDtypeStruct((cl, rows), bf),
            jax.ShapeDtypeStruct((CR, F // L), f32),
            jax.ShapeDtypeStruct((CR, F // L), f32),
            jax.ShapeDtypeStruct((TAPS, cl), f32),
        ),
        in_specs=[pl.BlockSpec(memory_space=pltpu.HBM)] * 5,
        out_specs=(vmem,) * 5,
        scratch_shapes=scratch,
        compiler_params=pltpu.CompilerParams(
            collective_id=0, has_side_effects=True, vmem_limit_bytes=50 * 1024 * 1024),
        cost_estimate=pl.CostEstimate(flops=12 * N * C * F, bytes_accessed=8 * rows * cl * 2, transcendentals=N * F),
    )(features.T, cotangent.T, kernel_tap_rows, in_weight, out_weight)
    return bo.T, gx.T, gw_in, gw_out.T, gk


def solution(mesh):
    placed = (P("loop", "chan"), P(None, "chan"), P(), P(), P("loop", "chan"))
    return jax.shard_map(
        fused_shards,
        mesh=mesh,
        in_specs=placed,
        out_specs=(
            P("loop", "chan"),
            P("loop", "chan"),
            P("chan", "loop"),
            P("loop", "chan"),
            P(None, "chan"),
        ),
        check_vma=False,
    )
```

```python
import functools
import math

import jax
import jax.numpy as jnp
from jax import lax
from jax.experimental import pallas as pl
from jax.experimental.pallas import tpu as pltpu
from jax.sharding import PartitionSpec as P

TAPS = 9
DILATION_STEP = 512


gelu_scale = math.sqrt(2.0 / math.pi)
cubic_coef = 0.044715
epsilon = 1e-05


def with_halo(cells, sides, width):
    for axis, dim in sides:
        count = lax.axis_size(axis)
        head = lax.slice_in_dim(cells, 0, width, axis=dim)
        tail = lax.slice_in_dim(cells, cells.shape[dim] - width, cells.shape[dim], axis=dim)
        cells = jnp.concatenate(
            [
                lax.ppermute(tail, axis, [(i, (i + 1) % count) for i in range(count)]),
                cells,
                lax.ppermute(head, axis, [((i + 1) % count, i) for i in range(count)]),
            ],
            axis=dim,
        )
    return cells


def gelu_pair(inputs):
    inner_arg = gelu_scale * (inputs + cubic_coef * inputs * inputs * inputs)
    tangent = jnp.tanh(inner_arg)
    act_value = 0.5 * inputs * (1.0 + tangent)
    act_slope = 0.5 * (1.0 + tangent) + 0.5 * inputs * (1.0 - tangent * tangent) * gelu_scale * (
        1.0 + 3.0 * cubic_coef * inputs * inputs
    )
    return (act_value, act_slope)


def widen_rows(field_rows, reach_positions):
    return with_halo(field_rows, (("loop", 0),), reach_positions)


def shards(features, kernel_tap_rows, in_weight, out_weight, cotangent):
    middle_position = (TAPS - 1) // 2
    reach_positions = middle_position * DILATION_STEP
    loop_size = lax.axis_size("loop")
    chan_size = lax.axis_size("chan")
    rows_here = features.shape[0]
    grad_scale = 1.0 / math.sqrt(rows_here * loop_size)
    padded_in = widen_rows(features, reach_positions)
    blended_sum = jnp.zeros(features.shape, jnp.float32)
    for kernel_tap_index in range(TAPS):
        leading_row = reach_positions + (kernel_tap_index - middle_position) * DILATION_STEP
        blended_sum = blended_sum + kernel_tap_rows[kernel_tap_index] * padded_in[
            leading_row : leading_row + rows_here
        ].astype(jnp.float32)
    filtered = blended_sum.astype(jnp.bfloat16)
    row_block, upstream = (
        lax.all_to_all(filtered, "chan", split_axis=0, concat_axis=1, tiled=True),
        lax.all_to_all(cotangent, "chan", split_axis=0, concat_axis=1, tiled=True),
    )
    values = row_block.astype(jnp.float32)
    mean_value = jnp.mean(values, axis=-1, keepdims=True)
    centred = values - mean_value
    variance = jnp.mean(centred * centred, axis=-1, keepdims=True)
    inv_std = lax.rsqrt(variance + epsilon)
    normed = centred * inv_std
    normed_b = normed.astype(jnp.bfloat16)
    hidden_pre = jnp.dot(normed_b, in_weight, preferred_element_type=jnp.float32)
    act_value, act_slope = gelu_pair(hidden_pre)
    act_b = act_value.astype(jnp.bfloat16)
    branch = jnp.dot(act_b, out_weight, preferred_element_type=jnp.float32).astype(jnp.bfloat16)
    grad_act = jnp.einsum("pc,fc->pf", upstream, out_weight, preferred_element_type=jnp.float32)
    grad_pre = (grad_act * act_slope).astype(jnp.bfloat16)
    grad_normed = jnp.einsum("pf,cf->pc", grad_pre, in_weight, preferred_element_type=jnp.float32)
    grad_filtered = inv_std * (
        grad_normed
        - jnp.mean(grad_normed, axis=-1, keepdims=True)
        - normed * jnp.mean(grad_normed * normed, axis=-1, keepdims=True)
    )
    back_rows = grad_filtered.astype(jnp.bfloat16)
    local_rows = row_block.shape[0]
    width_c = row_block.shape[1]
    width_f = hidden_pre.shape[1]
    chan_part = width_c // chan_size
    loop_part = width_f // loop_size
    normed_parts = normed_b.reshape(local_rows, chan_size, chan_part)
    upstream_parts = upstream.reshape(local_rows, chan_size, chan_part)
    grad_parts = grad_pre.reshape(local_rows, loop_size, loop_part)
    act_parts = act_b.reshape(local_rows, loop_size, loop_part)
    term_in = (
        jnp.einsum("pai,pbj->baij", normed_parts, grad_parts, preferred_element_type=jnp.float32)
        * grad_scale
    )
    term_out = (
        jnp.einsum("pbj,pai->baji", act_parts, upstream_parts, preferred_element_type=jnp.float32)
        * grad_scale
    )
    branch_cols, back_cols = (
        lax.all_to_all(branch, "chan", split_axis=1, concat_axis=0, tiled=True),
        lax.all_to_all(back_rows, "chan", split_axis=1, concat_axis=0, tiled=True),
    )
    block_out = (features.astype(jnp.float32) + branch_cols.astype(jnp.float32)).astype(
        jnp.bfloat16
    )
    first_in, first_out = (
        lax.psum_scatter(
            term_in.astype(jnp.bfloat16), "chan", scatter_dimension=1, tiled=True
        ).astype(jnp.float32),
        lax.psum_scatter(
            term_out.astype(jnp.bfloat16), "chan", scatter_dimension=1, tiled=True
        ).astype(jnp.float32),
    )
    summed_in, summed_out = (
        lax.psum_scatter(first_in, "loop", scatter_dimension=0, tiled=True),
        lax.psum_scatter(first_out, "loop", scatter_dimension=0, tiled=True),
    )
    grad_in_weight = summed_in.reshape(chan_part, loop_part)
    grad_out_weight = summed_out.reshape(loop_part, chan_part)
    padded_back = widen_rows(back_cols, reach_positions)
    grad_sum_rows = cotangent.astype(jnp.float32)
    back_wide = back_cols.astype(jnp.float32)
    kernel_rows = []
    for kernel_tap_index in range(TAPS):
        shift_positions = (kernel_tap_index - middle_position) * DILATION_STEP
        first_back = reach_positions - shift_positions
        grad_sum_rows = grad_sum_rows + kernel_tap_rows[kernel_tap_index] * padded_back[
            first_back : first_back + rows_here
        ].astype(jnp.float32)
        first_in_row = reach_positions + shift_positions
        kernel_rows.append(
            jnp.sum(
                back_wide * padded_in[first_in_row : first_in_row + rows_here].astype(jnp.float32),
                axis=0,
            )
        )
    kernel_terms = jnp.stack(kernel_rows) * grad_scale
    grad_kernel = lax.psum(kernel_terms, "loop")
    return (
        block_out,
        grad_sum_rows.astype(jnp.bfloat16),
        grad_in_weight,
        grad_out_weight,
        grad_kernel,
    )


MESH = pl.DeviceIdType.MESH
MIDDLE = (TAPS - 1) // 2
TILE_STEPS = 2


def fused_kernel(
    L, J, grad_scale,
    x, ct, taps, win, wout,
    bo_out, gx_out, gw_in_out, gw_out_out, gk_out,
    tb, tf, wint, woutt, xs, xe, cs, ctf, xr, nb, nrm, istd, act, gp, ge,
    bs, br, gs, gr, gfull, gsend, grecv, hf, hs, hr, sf, tr, kp, kr, kt,
    send, recv,
):
    cl, rows = x.shape
    C = cl * J
    F = win.shape[1]
    R = DILATION_STEP // J
    K = rows // DILATION_STEP
    PAIRS = K // 2
    TILE = 2 * R
    Z = L // 2
    own = MIDDLE * R
    me_l, me_j = lax.axis_index("loop"), lax.axis_index("chan")
    core, z = lax.rem(me_l, 2), me_l // 2
    used = [0]

    def take(n=1):
        used[0] += n
        return used[0] - n

    def rcopy(src, dst, idx, l, j):
        return pltpu.make_async_remote_copy(
            src_ref=src, dst_ref=dst, send_sem=send.at[idx], recv_sem=recv.at[idx],
            device_id=(l, j), device_id_type=MESH)

    chan_peers = [lax.rem(me_j + d, J) for d in range(1, J)]
    loop_peers = [lax.rem(me_l + e, L) for e in range(1, L)]
    right, left = loop_peers[0], loop_peers[-1]

    barrier = pltpu.get_barrier_semaphore()
    for j in chan_peers:
        pl.semaphore_signal(barrier, inc=1, device_id=(me_l, j), device_id_type=MESH)
    for l in loop_peers:
        pl.semaphore_signal(barrier, inc=1, device_id=(l, me_j), device_id_type=MESH)

    def pack(src, dst):
        for k in range(K):
            for j in range(J):
                a = k * DILATION_STEP + j * R
                dst[j, :, k * R:(k + 1) * R] = src[:, a:a + R]

    tb[me_j] = jnp.zeros((16, 128), jnp.float32)
    tb[me_j, 0:TAPS, 0:cl] = taps[...]
    pack(x, xs)
    pl.semaphore_wait(barrier, J - 1 + L - 1)

    pending = []

    def to_chan(src, dst):
        out = []
        for j in chan_peers:
            c = rcopy(src.at[j], dst.at[me_j], take(), me_l, j)
            c.start()
            out.append(c)
        pending.extend(out)
        return out

    x_in = to_chan(xs, xr)
    tap_in = []
    for j in chan_peers:
        c = rcopy(tb.at[me_j], tb.at[me_j], take(), me_l, j)
        c.start()
        tap_in.append(c)
    pending.extend(tap_in)
    pack(ct, cs)
    ct_in = to_chan(cs, ctf)

    wint[...] = win[...].T
    woutt[...] = wout[...].T
    xr[me_j] = xs[me_j]
    for c in x_in:
        c.wait_recv()
    for s in range(J):
        xe[s * cl:(s + 1) * cl, own:own + K * R] = xr[s]
    x_left = rcopy(xe.at[:, own:own + own], xe.at[:, own + K * R:2 * own + K * R], take(), left, me_j)
    x_left.start()
    x_right = rcopy(xe.at[:, K * R:own + K * R], xe.at[:, 0:own], take(), right, me_j)
    x_right.start()
    for c in tap_in:
        c.wait_recv()
    columns = jnp.concatenate(
        [jnp.concatenate([tb[s, :, 0:cl] for s in range(J)], axis=1), jnp.zeros((112, C), jnp.float32)], axis=0).T
    for t in range(TAPS):
        tf[t] = jnp.broadcast_to(columns[:, t:t + 1], (C, R))
    ctf[me_j] = cs[me_j]
    for c in ct_in:
        c.wait_recv()
    x_left.wait_recv()
    x_right.wait_recv()
    pending.extend([x_left, x_right])

    bo_base = take(PAIRS * (J - 1))
    ge_left = rcopy(ge.at[:, own:own + own], ge.at[:, own + K * R:2 * own + K * R], take(), left, me_j)
    ge_right = rcopy(ge.at[:, K * R:own + K * R], ge.at[:, 0:own], take(), right, me_j)
    gs_base = take(PAIRS * (J - 1))
    core_base = take(Z)

    def tile_sends(src, dst, base, tile):
        at = pl.ds(pl.multiple_of(tile * TILE, TILE), TILE)
        return [rcopy(src.at[j, :, at], dst.at[me_j, :, at], base + tile * (J - 1) + d, me_l, j)
                for d, j in enumerate(chan_peers)]

    def tile_body(tile, carry):
        base = pl.multiple_of(tile * TILE, TILE)
        for b in range(TILE_STEPS):
            for j in range(J):
                ch = slice(j * cl, (j + 1) * cl)
                acc = jnp.zeros((cl, R), jnp.float32)
                for t in range(TAPS):
                    acc = acc + tf[t, ch, :] * xe[ch, pl.ds(base + (b + t) * R, R)].astype(jnp.float32)
                nrm[ch, b * R:(b + 1) * R] = acc.astype(jnp.bfloat16).astype(jnp.float32)
            here_b = slice(b * R, (b + 1) * R)
            v = nrm[:, here_b]
            centred = v - jnp.mean(v, axis=0, keepdims=True)
            inv = lax.rsqrt(jnp.mean(centred * centred, axis=0, keepdims=True) + epsilon)
            normed = centred * inv
            nrm[:, here_b] = normed
            istd[:, here_b] = inv
            nb[:, pl.ds(base + b * R, R)] = normed.astype(jnp.bfloat16)
        here = pl.ds(base, TILE)
        normed_b = nb[:, here]
        up = jnp.concatenate([ctf[j, :, here] for j in range(J)], axis=0)
        FC = 256
        for f in range(F // FC):
            part = slice(f * FC, (f + 1) * FC)
            pre = jnp.dot(wint[part, :], normed_b, preferred_element_type=jnp.float32)
            ga = jnp.dot(wout[part, :], up, preferred_element_type=jnp.float32)
            sq = pre * pre
            tangent = jnp.tanh(pre * (gelu_scale + (gelu_scale * cubic_coef) * sq))
            gate = 0.5 + 0.5 * tangent
            slope = gate + pre * (gate * (1.0 - tangent)) * (gelu_scale + (3.0 * gelu_scale * cubic_coef) * sq)
            act[part, here] = (pre * gate).astype(jnp.bfloat16)
            gp[part, here] = (ga * slope).astype(jnp.bfloat16)
        gn = jnp.dot(win[...], gp[:, here], preferred_element_type=jnp.float32)
        for b in range(TILE_STEPS):
            s = slice(b * R, (b + 1) * R)
            g, normed = gn[:, s], nrm[:, s]
            out = istd[:, s] * (g - jnp.mean(g, axis=0, keepdims=True)
                                - normed * jnp.mean(g * normed, axis=0, keepdims=True))
            ge[:, pl.ds(own + base + b * R, R)] = out.astype(jnp.bfloat16)

        @pl.when(tile == PAIRS // 2 - 1)
        def _():
            ge_left.start()

        @pl.when(tile == PAIRS - 1)
        def _():
            ge_right.start()

        branch = jnp.dot(woutt[...], act[:, here], preferred_element_type=jnp.float32).astype(jnp.bfloat16)
        bo = (xe[:, pl.ds(own + base, TILE)].astype(jnp.float32) + branch.astype(jnp.float32)).astype(jnp.bfloat16)
        for j in range(J):
            bs[j, :, here] = bo[j * cl:(j + 1) * cl]
        for c in tile_sends(bs, br, bo_base, tile):
            c.start()
        return carry

    lax.fori_loop(0, PAIRS, tile_body, 0)

    def term_body(zz, carry):
        cols = pl.ds(pl.multiple_of(zz * 256, 256), 256)
        both = jnp.concatenate([ctf[j] for j in range(J)], axis=0)
        for i, (a, b) in enumerate(((nb[...], gp), (both, act))):
            term = lax.dot_general(a, b[cols, :], (((1,), (1,)), ((), ())),
                                   preferred_element_type=jnp.float32) * grad_scale
            for h in range(2):
                part = term[:, h * 128:(h + 1) * 128]
                gfull[h, zz, i] = part
                gsend[h, zz, i] = part.astype(jnp.bfloat16)
        rcopy(gsend.at[1 - core, zz], grecv.at[zz], core_base + zz, z * 2 + 1 - core, me_j).start()
        return carry

    lax.fori_loop(0, Z, term_body, 0)

    ge_left.wait_recv()
    ge_right.wait_recv()
    pending.extend([ge_left, ge_right])

    def back_body(tile, carry):
        base = pl.multiple_of(tile * TILE, TILE)
        for h in range(TILE_STEPS):
            off = base + h * R
            for j in range(J):
                ch = slice(j * cl, (j + 1) * cl)
                acc = ctf[j, :, pl.ds(off, R)].astype(jnp.float32)
                for t in range(TAPS):
                    acc = acc + tf[t, ch, :] * ge[ch, pl.ds(off + (TAPS - 1 - t) * R, R)].astype(jnp.float32)
                gs[j, :, pl.ds(off, R)] = acc.astype(jnp.bfloat16)
        for c in tile_sends(gs, gr, gs_base, tile):
            c.start()
        return carry

    lax.fori_loop(0, PAIRS, back_body, 0)

    for j in range(J):
        ch = slice(j * cl, (j + 1) * cl)
        sums = []
        for t in range(TAPS):
            acc = jnp.zeros((cl, R), jnp.float32)
            for k in range(K):
                acc = acc + (ge[ch, own + k * R:own + (k + 1) * R].astype(jnp.float32)
                             * xe[ch, (k + t) * R:(k + t + 1) * R].astype(jnp.float32))
            sums.append(jnp.sum(acc, axis=1, keepdims=True) * grad_scale)
        kp[j] = jnp.concatenate(sums + [jnp.zeros((cl, 128 - TAPS), jnp.float32)], axis=1)
    k_in = to_chan(kp, kr)

    CR = C // J

    def core_sum(zz, carry):
        c = rcopy(gsend.at[1 - core, zz], grecv.at[zz], core_base + zz, z * 2 + 1 - core, me_j)
        c.wait_recv()
        c.wait_send()
        for i in range(2):
            h = gfull[core, zz, i] + grecv[zz, i].astype(jnp.float32)
            for j in range(J):
                hf[j, zz, i] = h[j * CR:(j + 1) * CR]
                hs[j, zz, i] = h[j * CR:(j + 1) * CR].astype(jnp.bfloat16)
        return carry

    lax.fori_loop(0, Z, core_sum, 0)
    h_in = to_chan(hs, hr)
    for c in k_in:
        c.wait_recv()
    total = kp[me_j]
    for d in range(1, J):
        total = total + kr[lax.rem(me_j + J - d, J)]
    kt[me_l] = total
    kt_in = []
    for l in loop_peers:
        c = rcopy(kt.at[me_l], kt.at[me_l], take(), l, me_j)
        c.start()
        kt_in.append(c)
    pending.extend(kt_in)

    def finish(src, buf, base, out):
        buf[me_j] = src[me_j]
        for tile in range(PAIRS):
            for c in tile_sends(src, buf, base, tile):
                c.wait_recv()
                c.wait_send()
        for s in range(J):
            for k in range(K):
                at = k * DILATION_STEP + s * R
                out[:, at:at + R] = buf[s, :, k * R:(k + 1) * R]

    finish(bs, br, bo_base, bo_out)
    for c in h_in:
        c.wait_recv()
    for zz in range(Z):
        total = hf[me_j, zz]
        for d in range(1, J):
            total = total + hr[lax.rem(me_j + J - d, J), zz].astype(jnp.float32)
        sf[zz] = total
    z_in = []
    for e in range(1, Z):
        zz = lax.rem(z + e, Z)
        c = rcopy(sf.at[zz], tr.at[z], take(), zz * 2 + core, me_j)
        c.start()
        z_in.append(c)
    pending.extend(z_in)
    finish(gs, gr, gs_base, gx_out)
    for c in kt_in:
        c.wait_recv()
    total = kt[0]
    for l in range(1, L):
        total = total + kt[l]
    gk_out[...] = total.T[0:TAPS, :]
    for c in z_in:
        c.wait_recv()
    total = sf[z]
    for e in range(1, Z):
        total = total + tr[lax.rem(z + Z - e, Z)]
    gw_in_out[...] = total[0]
    gw_out_out[...] = total[1]
    for c in pending:
        c.wait_send()


def fits(L, J, rows, cl, F):
    R = DILATION_STEP // J
    return (cl * 2 == 128 and rows == 2 * MIDDLE * DILATION_STEP and L % 2 == 0 and L > 2 and J > 1
            and F == L * 128 and R == 128)


def fused_shards(features, kernel_tap_rows, in_weight, out_weight, cotangent):
    L, J = lax.axis_size("loop"), lax.axis_size("chan")
    rows, cl = features.shape
    C, F = in_weight.shape
    if not fits(L, J, rows, cl, F):
        return shards(features, kernel_tap_rows, in_weight, out_weight, cotangent)
    R = DILATION_STEP // J
    K = rows // DILATION_STEP
    N = K * R
    Z = L // 2
    CR = C // J
    bf, f32 = jnp.bfloat16, jnp.float32
    ext = N + 2 * MIDDLE * R
    packed = pltpu.VMEM((J, cl, N), bf)
    scratch = [
        pltpu.VMEM((J, 16, 128), f32),
        pltpu.VMEM((TAPS, C, R), f32),
        pltpu.VMEM((F, C), bf),
        pltpu.VMEM((C, F), bf),
        packed,
        pltpu.VMEM((C, ext), bf),
        packed, packed, packed,
        pltpu.VMEM((C, N), bf),
        pltpu.VMEM((C, 2 * R), f32),
        pltpu.VMEM((1, 2 * R), f32),
        pltpu.VMEM((F, N), bf),
        pltpu.VMEM((F, N), bf),
        pltpu.VMEM((C, ext), bf),
        packed, packed,
        packed, packed,
        pltpu.VMEM((2, Z, 2, C, 128), f32),
        pltpu.VMEM((2, Z, 2, C, 128), bf),
        pltpu.VMEM((Z, 2, C, 128), bf),
        pltpu.VMEM((J, Z, 2, CR, 128), f32),
        pltpu.VMEM((J, Z, 2, CR, 128), bf),
        pltpu.VMEM((J, Z, 2, CR, 128), bf),
        pltpu.VMEM((Z, 2, CR, 128), f32),
        pltpu.VMEM((Z, 2, CR, 128), f32),
        pltpu.VMEM((J, cl, 128), f32),
        pltpu.VMEM((J, cl, 128), f32),
        pltpu.VMEM((L, cl, 128), f32),
    ]
    copies = (J - 1) * 5 + 4 + 2 * (K // 2) * (J - 1) + Z + (L - 1) + (Z - 1)
    scratch += [pltpu.SemaphoreType.DMA((copies,)), pltpu.SemaphoreType.DMA((copies,))]
    vmem = pl.BlockSpec(memory_space=pltpu.VMEM)
    bo, gx, gw_in, gw_out, gk = pl.pallas_call(
        functools.partial(fused_kernel, L, J, 1.0 / math.sqrt(rows * L)),
        out_shape=(
            jax.ShapeDtypeStruct((cl, rows), bf),
            jax.ShapeDtypeStruct((cl, rows), bf),
            jax.ShapeDtypeStruct((CR, F // L), f32),
            jax.ShapeDtypeStruct((CR, F // L), f32),
            jax.ShapeDtypeStruct((TAPS, cl), f32),
        ),
        in_specs=[vmem] * 5,
        out_specs=(vmem,) * 5,
        scratch_shapes=scratch,
        compiler_params=pltpu.CompilerParams(
            collective_id=0, has_side_effects=True, vmem_limit_bytes=50 * 1024 * 1024),
        cost_estimate=pl.CostEstimate(flops=12 * N * C * F, bytes_accessed=8 * rows * cl * 2, transcendentals=N * F),
    )(features.T, cotangent.T, kernel_tap_rows, in_weight, out_weight)
    return bo.T, gx.T, gw_in, gw_out.T, gk


def solution(mesh):
    placed = (P("loop", "chan"), P(None, "chan"), P(), P(), P("loop", "chan"))
    return jax.shard_map(
        fused_shards,
        mesh=mesh,
        in_specs=placed,
        out_specs=(
            P("loop", "chan"),
            P("loop", "chan"),
            P("chan", "loop"),
            P("loop", "chan"),
            P(None, "chan"),
        ),
        check_vma=False,
    )
```
